128 devices in a mesh: rows: 16 (over y, z), cols: 8 (over x, core).
Axes of the slice: x: 4, y: 4, z: 4, core: 2. Of those that a mesh axis runs over, the one named last changes fastest.
Arguments:
- tile_values: float32 [16, 8, 320, 128, 128], P('rows', 'cols'), may hold values from -3.2 to 3.2
- tile_rows: int32 [16, 8, 320], P('rows', 'cols'), may hold values from 0 to 63
- tile_cols: int32 [16, 8, 320], P('rows', 'cols'), may hold values from 0 to 127
- tile_count: int32 [16, 8], P('rows', 'cols'), may hold values from 1 to 320, as said below
- probes: float32 [131072, 128], P(('rows', 'cols')), may hold values from -6.1 to 6.1
Outputs:
- basis: float32 [131072, 128], P(('rows', 'cols'))
- factor: float32 [128, 128], replicated
- first_factor: float32 [128, 128], replicated
The draws below stay inside these ranges and needn't reach their ends.
Inputs may be any that keep to these rules, and one draw needn't show every extreme that they name: `tile_count`: counts are skewed; at least one device has all 320 slots live in every draw.
All inputs are finite; a program needn't handle non-finite values.
Results may differ from the reference program's by a relative error of at most 0.0005.
Values sent between devices are 32-bit elements; how exact they have to be, the bound alone decides.
A program may use at most 192 MiB of HBM per device.

```python
import jax
import jax.numpy as jnp
from jax import lax

TILE = 128
PROBES = 128
ROWS_DEV = 1024
CAP = 320
NODES = 131072
PANEL_BLOCKS = 64
COL_BLOCKS = 128
N_ROWS = 16
N_COLS = 8


def draw_tile_values(key, part):
    key = jax.random.fold_in(key, 41)
    shape = (N_ROWS, N_COLS, CAP, TILE, TILE)
    position = jnp.arange(N_ROWS, dtype=jnp.float32) / max(N_ROWS - 1, 1)
    entries = jnp.clip(jax.random.normal(key, shape, jnp.float32), -4.0, 4.0)
    panel_scale = jnp.exp(position * 0.916)
    scaled = entries * panel_scale[:, None, None, None, None] / TILE ** 0.5
    return scaled.astype(jnp.float32)


def draw_tile_count(key, part):
    first_key, second_key = jax.random.split(jax.random.fold_in(key, 17))
    base = jax.random.randint(first_key, (N_ROWS * N_COLS,), 0, CAP + 1)
    counts = jnp.maximum(1, base * base // CAP)
    chosen = jax.random.randint(second_key, (), 0, N_ROWS * N_COLS)
    counts = jnp.where(jnp.arange(N_ROWS * N_COLS) == chosen, CAP, counts)
    return counts.reshape(N_ROWS, N_COLS).astype(jnp.int32)


def draw_probes(key, part):
    subkeys = jax.random.split(jax.random.fold_in(key, 29), 3)
    column_mix = jax.random.uniform(subkeys[1], (1, PROBES), jnp.float32, 0.5, 1.5)
    common = jnp.clip(jax.random.normal(subkeys[0], (NODES, 1), jnp.float32), -4.0, 4.0)
    jitter = jnp.clip(jax.random.normal(subkeys[2], (NODES, PROBES), jnp.float32), -4.0, 4.0)
    spread = PROBES ** 0.5 / 800.0
    return (common * column_mix + spread * jitter).astype(jnp.float32)


def plant(values, key, least, largest):
    longest = values.shape.index(max(values.shape))
    spots = []
    for shift in (0, 1):
        where = [jax.random.randint(jax.random.fold_in(key, axis), (), 0, length) for axis, length in enumerate(values.shape)]
        where[longest] = (where[longest] + shift) % values.shape[longest]
        spots.append(tuple(where))
    return values.at[spots[0]].set(least).at[spots[1]].set(largest)


def setup_inputs(seed: int = 0) -> dict:
    splits = jax.random.split(jax.random.key(seed), 6)
    tile_values = draw_tile_values(jax.random.fold_in(splits[5], 71), 0)
    tile_rows = plant(jax.random.randint(splits[1], (N_ROWS, N_COLS, CAP), 0, PANEL_BLOCKS), jax.random.fold_in(splits[1], 1), 0, PANEL_BLOCKS - 1).astype(jnp.int32)
    tile_cols = plant(jax.random.randint(splits[2], (N_ROWS, N_COLS, CAP), 0, COL_BLOCKS), jax.random.fold_in(splits[2], 1), 0, COL_BLOCKS - 1).astype(jnp.int32)
    tile_count = draw_tile_count(jax.random.fold_in(splits[5], 71), 0)
    probes = draw_probes(jax.random.fold_in(splits[5], 71), 0)
    return {"tile_values": tile_values, "tile_rows": tile_rows, "tile_cols": tile_cols, "tile_count": tile_count, "probes": probes}


def panel_partial(tiles, rows_idx, cols_idx, count, columns):
    blocks = columns.reshape(-1, TILE, PROBES)
    picked = jnp.take(blocks, cols_idx, axis=0)
    products = jnp.einsum('cij,cjk->cik', tiles, picked, precision=lax.Precision.HIGHEST)
    slots = jnp.arange(tiles.shape[0], dtype=jnp.int32)
    live = slots < count
    onehot = ((rows_idx[None, :] == jnp.arange(PANEL_BLOCKS, dtype=jnp.int32)[:, None]) & live[None, :]).astype(tiles.dtype)
    return jnp.einsum('pc,cik->pik', onehot, products, precision=lax.Precision.HIGHEST).reshape(-1, PROBES)

def orthogonal(matrix):
    gram = jnp.einsum('rk,rl->kl', matrix, matrix, precision=lax.Precision.HIGHEST) / NODES
    lower = jnp.linalg.cholesky(gram)
    inverse = jax.scipy.linalg.solve_triangular(lower, jnp.eye(PROBES, dtype=matrix.dtype), lower=True)
    return (jnp.dot(matrix, inverse.T, precision=lax.Precision.HIGHEST), lower)

def reference(tile_values, tile_rows, tile_cols, tile_count, probes):
    groups = probes.reshape(N_ROWS, N_COLS, ROWS_DEV, PROBES)

    def one_panel(row_panel):

        def add(column, total):
            columns = lax.dynamic_index_in_dim(groups, column, axis=1, keepdims=False).reshape(-1, PROBES)
            return total + panel_partial(tile_values[row_panel, column], tile_rows[row_panel, column], tile_cols[row_panel, column], tile_count[row_panel, column], columns)
        return lax.fori_loop(0, N_COLS, add, jnp.zeros((PANEL_BLOCKS * TILE, PROBES), dtype=probes.dtype))
    product = lax.map(one_panel, jnp.arange(N_ROWS, dtype=jnp.int32)).reshape(NODES, PROBES)
    first, lower = orthogonal(product)
    basis, lower2 = orthogonal(first)
    factor = jnp.dot(lower2.T, lower.T, precision=lax.Precision.HIGHEST)
    return (basis, factor, lower.T)
```

```python
import jax
import jax.numpy as jnp
from jax import lax
from jax.experimental import pallas as pl
from jax.experimental.pallas import tpu as pltpu
from jax.sharding import PartitionSpec as P

N_ROWS = 16
N_COLS = 8
MESH = pl.DeviceIdType.MESH


def panel_partial(tiles, rows_idx, cols_idx, count, columns, panel_blocks):
    tile_size = tiles.shape[1]
    width = columns.shape[1]
    blocks = columns.reshape(-1, tile_size, width)
    picked = jnp.take(blocks, cols_idx, axis=0)
    products = jnp.einsum("cij,cjk->cik", tiles, picked, precision=lax.Precision.HIGHEST)
    slots = jnp.arange(tiles.shape[0], dtype=jnp.int32)
    live = slots < count
    onehot = (
        (rows_idx[None, :] == jnp.arange(panel_blocks, dtype=jnp.int32)[:, None]) & live[None, :]
    ).astype(tiles.dtype)
    return jnp.einsum("pc,cik->pik", onehot, products, precision=lax.Precision.HIGHEST).reshape(
        -1, width
    )


def local_gram(matrix):
    return jnp.einsum("rk,rl->kl", matrix, matrix, precision=lax.Precision.HIGHEST)


def triangle_inverse(gram, nodes):
    lower = jnp.linalg.cholesky(gram / nodes)
    inverse = jax.scipy.linalg.solve_triangular(
        lower, jnp.eye(gram.shape[0], dtype=gram.dtype), lower=True
    )
    return (lower, inverse)


def signal_all(sem, r, c):
    def cols_peer(d, carry):
        pl.semaphore_signal(sem, inc=1, device_id=(r, lax.rem(c + d, N_COLS)), device_id_type=MESH)
        return carry

    def rows_peer(d, carry):
        pl.semaphore_signal(sem, inc=1, device_id=(lax.rem(r + d, N_ROWS), c), device_id_type=MESH)
        return carry

    lax.fori_loop(1, N_COLS, cols_peer, 0)
    lax.fori_loop(1, N_ROWS, rows_peer, 0)


def sum_kernel(g_ref, out_ref, part, got_a, got_b, send_a, recv_a, send_b, recv_b, send_c, recv_c):
    r, c = lax.axis_index("rows"), lax.axis_index("cols")
    barrier = pltpu.get_barrier_semaphore()
    signal_all(barrier, r, c)
    pl.semaphore_wait(barrier, N_COLS - 1 + N_ROWS - 1)

    def copy_a(d):
        to = lax.rem(c + d, N_COLS)
        return pltpu.make_async_remote_copy(
            src_ref=g_ref.at[to], dst_ref=got_a.at[d], send_sem=send_a.at[d], recv_sem=recv_a.at[d],
            device_id=(r, to), device_id_type=MESH)

    def copy_b(d):
        return pltpu.make_async_remote_copy(
            src_ref=part, dst_ref=got_b.at[r], send_sem=send_b.at[d], recv_sem=recv_b.at[d],
            device_id=(lax.rem(r + d, N_ROWS), c), device_id_type=MESH)

    def copy_c(d):
        return pltpu.make_async_remote_copy(
            src_ref=out_ref.at[c], dst_ref=out_ref.at[c], send_sem=send_c.at[d], recv_sem=recv_c.at[d],
            device_id=(r, lax.rem(c + d, N_COLS)), device_id_type=MESH)

    def each(copy, n, act):
        def step(d, carry):
            getattr(copy(d), act)()
            return carry

        lax.fori_loop(1, n, step, 0)

    each(copy_a, N_COLS, "start")
    each(copy_a, N_COLS, "wait_recv")
    total = g_ref[c]
    for d in range(1, N_COLS):
        total = total + got_a[d]
    part[...] = total
    got_b[r] = total
    each(copy_b, N_ROWS, "start")
    each(copy_a, N_COLS, "wait_send")
    each(copy_b, N_ROWS, "wait_recv")
    total = got_b[0]
    for d in range(1, N_ROWS):
        total = total + got_b[d]
    out_ref[c] = total
    each(copy_c, N_COLS, "start")
    each(copy_b, N_ROWS, "wait_send")
    each(copy_c, N_COLS, "wait")


def sum_everywhere(matrix, ident):
    size = matrix.shape[0]
    rows = size // N_COLS
    piece = (rows, size)
    dma = pltpu.SemaphoreType.DMA
    out = pl.pallas_call(
        sum_kernel,
        out_shape=jax.ShapeDtypeStruct((N_COLS,) + piece, jnp.float32),
        in_specs=[pl.BlockSpec(memory_space=pltpu.VMEM)],
        out_specs=pl.BlockSpec(memory_space=pltpu.VMEM),
        scratch_shapes=[
            pltpu.VMEM(piece, jnp.float32),
            pltpu.VMEM((N_COLS,) + piece, jnp.float32),
            pltpu.VMEM((N_ROWS,) + piece, jnp.float32),
            dma((N_COLS,)), dma((N_COLS,)), dma((N_ROWS,)), dma((N_ROWS,)), dma((N_COLS,)), dma((N_COLS,)),
        ],
        compiler_params=pltpu.CompilerParams(collective_id=ident, has_side_effects=True),
        name="sum_everywhere",
    )(matrix.reshape((N_COLS,) + piece))
    return out.reshape(size, size)


def shards(tile_values, tile_rows, tile_cols, tile_count, probes):
    tiles = tile_values[0, 0]
    rows_idx = tile_rows[0, 0]
    cols_idx = tile_cols[0, 0]
    count = tile_count[0, 0]
    own_rows = probes.shape[0]
    tile_size = tiles.shape[1]
    nodes = own_rows * N_ROWS * N_COLS
    panel_blocks = N_COLS * own_rows // tile_size
    gathered = lax.all_gather(probes, "rows", axis=0, tiled=True)
    panel = panel_partial(tiles, rows_idx, cols_idx, count, gathered, panel_blocks)
    own = lax.psum_scatter(panel, "cols", scatter_dimension=0, tiled=True)
    gram = sum_everywhere(local_gram(own), 1)
    lower, inverse = triangle_inverse(gram, nodes)
    first = jnp.dot(own, inverse.T, precision=lax.Precision.HIGHEST)
    gram_next = sum_everywhere(local_gram(first), 1)
    lower_next, inverse_next = triangle_inverse(gram_next, nodes)
    basis = jnp.dot(first, inverse_next.T, precision=lax.Precision.HIGHEST)
    factor = jnp.dot(lower_next.T, lower.T, precision=lax.Precision.HIGHEST)
    return (basis, factor, lower.T)


def solution(mesh):
    placed = (
        P("rows", "cols", None, None, None),
        P("rows", "cols", None),
        P("rows", "cols", None),
        P("rows", "cols"),
        P(("rows", "cols"), None),
    )
    return jax.shard_map(
        shards,
        mesh=mesh,
        in_specs=placed,
        out_specs=(P(("rows", "cols"), None), P(), P()),
        check_vma=False,
    )
```

```python
import jax
import jax.numpy as jnp
from jax import lax
from jax.experimental import pallas as pl
from jax.experimental.pallas import tpu as pltpu
from jax.sharding import PartitionSpec as P

SIDE = 4
N_ROWS = SIDE * SIDE
N_COLS = 8
TILE = 128
CAP = 320
OWN = 8
PANEL = OWN * N_COLS
PARTS = 4
WIDTH = TILE // PARTS
GROUP = 32
STAGE = 8
SLOTS = 8
MESH = pl.DeviceIdType.MESH
DMA = pltpu.SemaphoreType.DMA


def halves(value):
    high = value.astype(jnp.bfloat16)
    low = (value - high.astype(jnp.float32)).astype(jnp.bfloat16)
    return high, low


def product_kernel(
    order, columns, last, keep, tiles, probes, out,
    own, gx, pairs, stage, xpair, sums, panel, near, mid, far,
    stage_sem, sa, ra, sb, rb, sc, rc, sd, rd, se, re, sf, rf, sg, rg,
):
    r, c = lax.axis_index("rows"), lax.axis_index("cols")
    y, z = r // SIDE, lax.rem(r, SIDE)
    x, q = c // 2, lax.rem(c, 2)

    def turn(v, off):
        return lax.rem(v + off + SIDE, SIDE)

    def yz(dim, off):
        return (turn(y, off), z) if dim == 0 else (y, turn(z, off))

    def row_peer(dim, off):
        yy, zz = yz(dim, off)
        return (yy * SIDE + zz, c)

    def x_peer(off):
        return (r, turn(x, off) * 2 + q)

    partner = (r, x * 2 + 1 - q)

    def load(i, slot):
        return pltpu.make_async_copy(tiles.at[pl.ds(i * STAGE, STAGE)], stage.at[slot], stage_sem.at[slot])

    for i in range(SLOTS):
        load(i, i).start()

    barrier = pltpu.get_barrier_semaphore()
    peers = [row_peer(dim, off) for dim in (0, 1) for off in (1, -1)] + [x_peer(1), x_peer(-1), partner]
    for peer in peers:
        pl.semaphore_signal(barrier, inc=1, device_id=peer, device_id_type=MESH)

    def turned(b, carry):
        block = jnp.transpose(probes[b])
        for j in range(PARTS):
            own[j, b] = block[j * WIDTH:(j + 1) * WIDTH]
            gx[j, y, z, b] = block[j * WIDTH:(j + 1) * WIDTH]
        return carry

    lax.fori_loop(0, OWN, turned, 0)
    pl.semaphore_wait(barrier, len(peers))

    def remote(src, dst, send, recv, to):
        return pltpu.make_async_remote_copy(
            src_ref=src, dst_ref=dst, send_sem=send, recv_sem=recv, device_id=to, device_id_type=MESH)

    def step_of(s):
        return 1 if s == 0 else -1

    def copy_a(j, h, s):
        return remote(own.at[j, pl.ds(4 * h, 4)], gx.at[j, y, z, pl.ds(4 * h, 4)],
                      sa.at[j, h, s], ra.at[j, h, s], row_peer(1 - h, step_of(s)))

    def copy_b(j, h, s):
        yy, zz = yz(1 - h, -step_of(s))
        ref = gx.at[j, yy, zz, pl.ds(4 * h + 2 * s, 2)]
        return remote(ref, ref, sb.at[j, h, s], rb.at[j, h, s], row_peer(1 - h, step_of(s)))

    def copy_c(j, h, s):
        ref = gx.at[j, y, :, pl.ds(4 * h, 4)] if h == 0 else gx.at[j, :, z, pl.ds(4 * h, 4)]
        return remote(ref, ref, sc.at[j, h, s], rc.at[j, h, s], row_peer(h, step_of(s)))

    def copy_d(j, h, s):
        yy, zz = yz(h, -step_of(s))
        cut = pl.ds(4 * h + 2 * s, 2)
        ref = gx.at[j, yy, :, cut] if h == 0 else gx.at[j, :, zz, cut]
        return remote(ref, ref, sd.at[j, h, s], rd.at[j, h, s], row_peer(h, step_of(s)))

    ways = [(h, s) for h in (0, 1) for s in (0, 1)]

    def do_a(j):
        for h, s in ways:
            copy_a(j, h, s).start()

    def do_b(j):
        for h, s in ways:
            copy_a(j, h, s).wait_recv()
            copy_b(j, h, s).start()

    def do_c(j):
        for h in (0, 1):
            copy_b(j, h, 0).wait_recv()
            copy_b(j, h, 1).wait_recv()
            copy_c(j, h, 0).start()
            copy_c(j, h, 1).start()

    def do_d(j):
        for h, s in ways:
            copy_c(j, h, s).wait_recv()
            copy_d(j, h, s).start()

    def do_e(j):
        for h, s in ways:
            copy_d(j, h, s).wait_recv()

    def split(i, carry):
        slot = lax.rem(i, SLOTS)
        load(i, slot).wait()
        for k in range(STAGE):
            high, low = halves(jnp.transpose(stage[slot, k]))
            pairs[i * STAGE + k, 0:TILE] = high
            pairs[i * STAGE + k, TILE:2 * TILE] = low

        @pl.when(i + SLOTS < CAP // STAGE)
        def _():
            load(i + SLOTS, slot).start()

        return carry

    def spread(j):
        def one(g, carry):
            high, low = halves(gx[j, g // 32, lax.rem(g // 8, 4), lax.rem(g, 8)])
            xpair[g, 0:WIDTH, 0:TILE] = high
            xpair[g, 0:WIDTH, TILE:2 * TILE] = high
            xpair[g, WIDTH:2 * WIDTH, 0:TILE] = low
            xpair[g, WIDTH:2 * WIDTH, TILE:2 * TILE] = low
            return carry

        lax.fori_loop(0, N_ROWS * OWN, one, 0, unroll=8)

    def multiply(first, count, run):
        def group(g, run):
            for u in range(GROUP):
                t = first + g * GROUP + u
                both = jnp.dot(xpair[columns[t]], pairs[order[t]], preferred_element_type=jnp.float32)
                run = run * keep[t] + (both[:WIDTH] + both[WIDTH:])
                sums[t] = run
            return run

        return lax.fori_loop(0, count // GROUP, group, run)

    def collect(j):
        def one(i, carry):
            at = last[i]
            panel[j, i // 16, lax.rem(i // 8, 2), lax.rem(i, 8)] = jnp.where(
                at >= 0, sums[jnp.maximum(at, 0)], 0.0)
            return carry

        lax.fori_loop(0, PANEL, one, 0, unroll=8)

    def swap(j):
        return remote(panel.at[j, :, 1 - q], near.at[j], se.at[j], re.at[j], partner)

    def copy_f(j, s):
        return remote(panel.at[j, turn(x, 2), q, pl.ds(4 * s, 4)], mid.at[j, s],
                      sf.at[j, s], rf.at[j, s], x_peer(step_of(s)))

    def copy_g(j, s):
        return remote(panel.at[j, turn(x, step_of(s)), q], far.at[j, s],
                      sg.at[j, s], rg.at[j, s], x_peer(step_of(s)))

    def do_p(j):
        collect(j)
        swap(j).start()

    def do_q(j):
        swap(j).wait_recv()
        for off in (2, 1, -1, 0):
            at = turn(x, off)
            panel[j, at, q] = panel[j, at, q] + near[j, at]
            if off == 2:
                copy_f(j, 0).start()
                copy_f(j, 1).start()

    def do_r(j):
        for s in (0, 1):
            copy_f(j, s).wait_recv()
            at = turn(x, step_of(s))
            cut = pl.ds(4 * s, 4)
            panel[j, at, q, cut] = panel[j, at, q, cut] + mid[j, s]
            copy_g(j, s).start()

    def do_s(j):
        copy_g(j, 0).wait_recv()
        copy_g(j, 1).wait_recv()
        out[:, j * WIDTH:(j + 1) * WIDTH, :] = panel[j, x, q] + (far[j, 0] + far[j, 1])

    steps = CAP // STAGE

    def some(lo, hi):
        lax.fori_loop(lo, hi, split, 0)

    for j in range(PARTS):
        do_a(j)
    some(0, 5)
    do_b(0)
    some(5, 8)
    do_b(1)
    some(8, 11)
    do_b(2)
    do_c(0)
    some(11, 15)
    do_b(3)
    do_c(1)
    some(15, 28)
    do_d(0)
    do_c(2)
    some(28, steps)
    do_e(0)

    zero = jnp.zeros((WIDTH, TILE), jnp.float32)
    cuts = (0, 64, 160, 224, 320)

    def part(j, between):
        spread(j)
        run = zero
        for k in range(4):
            run = multiply(cuts[k], cuts[k + 1] - cuts[k], run)
            for act, i in between[k]:
                act(i)

    part(0, [[(do_d, 1), (do_c, 3)], [], [], [(do_p, 0)]])
    do_e(1)
    part(1, [[(do_q, 0)], [(do_d, 2)], [], [(do_r, 0), (do_p, 1)]])
    do_e(2)
    part(2, [[(do_d, 3)], [(do_q, 1), (do_s, 0)], [], [(do_r, 1), (do_p, 2)]])
    do_e(3)
    part(3, [[], [(do_q, 2), (do_s, 1)], [], [(do_r, 2), (do_p, 3)]])
    do_q(3)
    do_s(2)
    do_r(3)
    do_s(3)
    for j in range(PARTS):
        for h, s in ways:
            for copy in (copy_a, copy_b, copy_c, copy_d):
                copy(j, h, s).wait_send()
        swap(j).wait_send()
        for s in (0, 1):
            copy_f(j, s).wait_send()
            copy_g(j, s).wait_send()


def sorted_slots(rows_idx, cols_idx, count):
    slots = jnp.arange(CAP, dtype=jnp.int32)
    key = jnp.where(slots < count, rows_idx, PANEL) * CAP + slots
    rank = jnp.sum((key[None, :] < key[:, None]).astype(jnp.int32), axis=1)
    chosen = rank[None, :] == slots[:, None]

    def pick(values):
        return jnp.sum(jnp.where(chosen, values[None, :], 0), axis=1)

    order = pick(slots)
    columns = pick(cols_idx)
    row = pick(key) // CAP
    keep = jnp.concatenate([jnp.zeros((1,), jnp.float32), (row[1:] == row[:-1]).astype(jnp.float32)])
    panels = jnp.arange(PANEL, dtype=jnp.int32)
    here = row[None, :] == panels[:, None]
    last = jnp.max(jnp.where(here, slots[None, :], -1), axis=1)
    return order, columns, last, keep


def product(tiles, rows_idx, cols_idx, count, probes):
    order, columns, last, keep = sorted_slots(rows_idx, cols_idx, count)
    scalar = pl.BlockSpec(memory_space=pltpu.SMEM)
    vector = pl.BlockSpec(memory_space=pltpu.VMEM)
    f32, bf16 = jnp.float32, jnp.bfloat16
    piece = (OWN, WIDTH, TILE)
    return pl.pallas_call(
        product_kernel,
        out_shape=jax.ShapeDtypeStruct((OWN, TILE, TILE), f32),
        in_specs=[scalar] * 4 + [pl.BlockSpec(memory_space=pl.ANY), vector],
        out_specs=vector,
        scratch_shapes=[
            pltpu.VMEM((PARTS,) + piece, f32),
            pltpu.VMEM((PARTS, SIDE, SIDE) + piece, f32),
            pltpu.VMEM((CAP, 2 * TILE, TILE), bf16),
            pltpu.VMEM((SLOTS, STAGE, TILE, TILE), f32),
            pltpu.VMEM((N_ROWS * OWN, 2 * WIDTH, 2 * TILE), bf16),
            pltpu.VMEM((CAP, WIDTH, TILE), f32),
            pltpu.VMEM((PARTS, SIDE, 2) + piece, f32),
            pltpu.VMEM((PARTS, SIDE) + piece, f32),
            pltpu.VMEM((PARTS, 2, OWN // 2, WIDTH, TILE), f32),
            pltpu.VMEM((PARTS, 2) + piece, f32),
            DMA((SLOTS,)),
        ]
        + [DMA((PARTS, 2, 2))] * 8
        + [DMA((PARTS,))] * 2
        + [DMA((PARTS, 2))] * 4,
        compiler_params=pltpu.CompilerParams(
            collective_id=2, has_side_effects=True, vmem_limit_bytes=60 * 2**20),
        name="product",
    )(order, columns, last, keep, tiles, probes.reshape(OWN, TILE, TILE))


def local_gram(matrix):
    return jnp.einsum("rk,rl->kl", matrix, matrix, precision=lax.Precision.HIGHEST)


def triangle_inverse(gram, nodes):
    lower = jnp.linalg.cholesky(gram / nodes)
    inverse = jax.scipy.linalg.solve_triangular(
        lower, jnp.eye(gram.shape[0], dtype=gram.dtype), lower=True
    )
    return (lower, inverse)


def signal_all(sem, r, c):
    def cols_peer(d, carry):
        pl.semaphore_signal(sem, inc=1, device_id=(r, lax.rem(c + d, N_COLS)), device_id_type=MESH)
        return carry

    def rows_peer(d, carry):
        pl.semaphore_signal(sem, inc=1, device_id=(lax.rem(r + d, N_ROWS), c), device_id_type=MESH)
        return carry

    lax.fori_loop(1, N_COLS, cols_peer, 0)
    lax.fori_loop(1, N_ROWS, rows_peer, 0)


def sum_kernel(g_ref, out_ref, part, got_a, got_b, send_a, recv_a, send_b, recv_b, send_c, recv_c):
    r, c = lax.axis_index("rows"), lax.axis_index("cols")
    barrier = pltpu.get_barrier_semaphore()
    signal_all(barrier, r, c)
    pl.semaphore_wait(barrier, N_COLS - 1 + N_ROWS - 1)

    def copy_a(d):
        to = lax.rem(c + d, N_COLS)
        return pltpu.make_async_remote_copy(
            src_ref=g_ref.at[to], dst_ref=got_a.at[d], send_sem=send_a.at[d], recv_sem=recv_a.at[d],
            device_id=(r, to), device_id_type=MESH)

    def copy_b(d):
        return pltpu.make_async_remote_copy(
            src_ref=part, dst_ref=got_b.at[r], send_sem=send_b.at[d], recv_sem=recv_b.at[d],
            device_id=(lax.rem(r + d, N_ROWS), c), device_id_type=MESH)

    def copy_c(d):
        return pltpu.make_async_remote_copy(
            src_ref=out_ref.at[c], dst_ref=out_ref.at[c], send_sem=send_c.at[d], recv_sem=recv_c.at[d],
            device_id=(r, lax.rem(c + d, N_COLS)), device_id_type=MESH)

    def each(copy, n, act):
        def step(d, carry):
            getattr(copy(d), act)()
            return carry

        lax.fori_loop(1, n, step, 0)

    each(copy_a, N_COLS, "start")
    each(copy_a, N_COLS, "wait_recv")
    total = g_ref[c]
    for d in range(1, N_COLS):
        total = total + got_a[d]
    part[...] = total
    got_b[r] = total
    each(copy_b, N_ROWS, "start")
    each(copy_a, N_COLS, "wait_send")
    each(copy_b, N_ROWS, "wait_recv")
    total = got_b[0]
    for d in range(1, N_ROWS):
        total = total + got_b[d]
    out_ref[c] = total
    each(copy_c, N_COLS, "start")
    each(copy_b, N_ROWS, "wait_send")
    each(copy_c, N_COLS, "wait")


def sum_everywhere(matrix, ident):
    size = matrix.shape[0]
    rows = size // N_COLS
    piece = (rows, size)
    dma = pltpu.SemaphoreType.DMA
    out = pl.pallas_call(
        sum_kernel,
        out_shape=jax.ShapeDtypeStruct((N_COLS,) + piece, jnp.float32),
        in_specs=[pl.BlockSpec(memory_space=pltpu.VMEM)],
        out_specs=pl.BlockSpec(memory_space=pltpu.VMEM),
        scratch_shapes=[
            pltpu.VMEM(piece, jnp.float32),
            pltpu.VMEM((N_COLS,) + piece, jnp.float32),
            pltpu.VMEM((N_ROWS,) + piece, jnp.float32),
            dma((N_COLS,)), dma((N_COLS,)), dma((N_ROWS,)), dma((N_ROWS,)), dma((N_COLS,)), dma((N_COLS,)),
        ],
        compiler_params=pltpu.CompilerParams(collective_id=ident, has_side_effects=True),
        name="sum_everywhere",
    )(matrix.reshape((N_COLS,) + piece))
    return out.reshape(size, size)


def shards(tile_values, tile_rows, tile_cols, tile_count, probes):
    tiles = tile_values[0, 0]
    rows_idx = tile_rows[0, 0]
    cols_idx = tile_cols[0, 0]
    count = tile_count[0, 0]
    own_rows = probes.shape[0]
    nodes = own_rows * N_ROWS * N_COLS
    blocks = product(tiles, rows_idx, cols_idx, count, probes)
    own = jnp.swapaxes(blocks, 1, 2).reshape(own_rows, TILE)
    gram = sum_everywhere(local_gram(own), 1)
    lower, inverse = triangle_inverse(gram, nodes)
    first = jnp.dot(own, inverse.T, precision=lax.Precision.HIGHEST)
    gram_next = sum_everywhere(local_gram(first), 1)
    lower_next, inverse_next = triangle_inverse(gram_next, nodes)
    basis = jnp.dot(first, inverse_next.T, precision=lax.Precision.HIGHEST)
    factor = jnp.dot(lower_next.T, lower.T, precision=lax.Precision.HIGHEST)
    return (basis, factor, lower.T)


def solution(mesh):
    placed = (
        P("rows", "cols", None, None, None),
        P("rows", "cols", None),
        P("rows", "cols", None),
        P("rows", "cols"),
        P(("rows", "cols"), None),
    )
    return jax.shard_map(
        shards,
        mesh=mesh,
        in_specs=placed,
        out_specs=(P(("rows", "cols"), None), P(), P()),
        check_vma=False,
    )
```

```python
import jax
import jax.numpy as jnp
from jax import lax
from jax.experimental import pallas as pl
from jax.experimental.pallas import tpu as pltpu
from jax.sharding import PartitionSpec as P

SIDE = 4
N_ROWS = SIDE * SIDE
N_COLS = 8
TILE = 128
CAP = 320
OWN = 8
PANEL = OWN * N_COLS
PARTS = 4
WIDTH = TILE // PARTS
GROUP = 32
STAGE = 8
STRIP = 16
SLICE = TILE // N_COLS
NODES = OWN * TILE * N_ROWS * N_COLS
SLOTS = 8
MESH = pl.DeviceIdType.MESH
DMA = pltpu.SemaphoreType.DMA


def halves(value):
    high = value.astype(jnp.bfloat16)
    low = (value - high.astype(jnp.float32)).astype(jnp.bfloat16)
    return high, low


def exact(left, right, at, to):
    return lax.dot_general(
        left, right, (((at,), (to,)), ((), ())), precision=lax.Precision.HIGHEST,
        preferred_element_type=jnp.float32)


def triangles(gram, upper, inverse, work):
    rows = lax.broadcasted_iota(jnp.int32, (TILE, TILE), 0)
    cols = lax.broadcasted_iota(jnp.int32, (TILE, TILE), 1)
    work[:, 0:TILE] = gram
    work[:, TILE:2 * TILE] = jnp.where(rows == cols, 1.0, 0.0)
    shape = (STRIP, TILE)
    place = lax.broadcasted_iota(jnp.int32, shape, 0)
    for lo in range(0, TILE, STRIP):
        hi = lo + STRIP
        strip = work[lo:hi, 0:TILE]
        turned = work[lo:hi, TILE:2 * TILE]
        columns = [jnp.broadcast_to(strip[:, lo + j:lo + j + 1], shape) for j in range(STRIP)]
        for k in range(STRIP):
            scale = lax.rsqrt(jnp.broadcast_to(columns[k][k:k + 1], shape))
            weight = columns[k] * scale
            for j in range(k + 1, STRIP):
                columns[j] = columns[j] - weight * jnp.broadcast_to(weight[j:j + 1], shape)
            pivot = jnp.broadcast_to(strip[k:k + 1], shape) * scale
            other = jnp.broadcast_to(turned[k:k + 1], shape) * scale
            weight = jnp.where(place > k, weight, 0.0)
            strip = jnp.where(place == k, pivot, strip - weight * pivot)
            turned = jnp.where(place == k, other, turned - weight * other)
        strip = jnp.where(cols[lo:hi] >= rows[lo:hi], strip, 0.0)
        upper[lo:hi, :] = strip
        inverse[lo:hi, :] = turned
        if hi < TILE:
            change = exact(strip, jnp.concatenate([strip, turned], axis=1), 0, 0)
            work[hi:, :] = work[hi:, :] - change[hi:, :]


def sort_slots(count, rows_idx, cols_idx, plan):
    blocks = CAP // TILE + 1
    square = (TILE, TILE)
    lane = lax.broadcasted_iota(jnp.int32, (1, TILE), 1)
    high = lax.broadcasted_iota(jnp.int32, square, 0)
    wide = lax.broadcasted_iota(jnp.int32, square, 1)

    def block(ref, b):
        width = min(TILE, CAP - b * TILE)
        value = ref[:, b * TILE:b * TILE + width]
        if width < TILE:
            value = jnp.concatenate([value, jnp.zeros((1, TILE - width), jnp.int32)], axis=1)
        return value

    def down(value):
        return jnp.transpose(jnp.broadcast_to(value, square))

    def total(mask, value=1):
        return jnp.sum(jnp.where(mask, value, 0), axis=0, keepdims=True)

    slot = [lane + b * TILE for b in range(blocks)]
    row = [jnp.where(slot[b] < count, block(rows_idx, b), PANEL) for b in range(blocks)]
    row_down = [down(v) for v in row]
    place, packed = [], []
    for b in range(blocks):
        rank = jnp.zeros((1, TILE), jnp.int32)
        before = jnp.zeros((1, TILE), jnp.int32)
        for a in range(blocks):
            same = row_down[a] == row[b]
            if a == b:
                same = jnp.logical_and(same, high < wide)
            earlier = row_down[a] < row[b]
            if a <= b:
                earlier = jnp.logical_or(earlier, same)
                before = before + total(same)
            rank = rank + total(earlier)
        place.append(down(rank))
        goes_on = jnp.where(before > 0, 1, 0)
        packed.append(down((goes_on * blocks * TILE + slot[b]) * TILE + block(cols_idx, b)))
    for b in range(blocks):
        value = jnp.zeros((1, TILE), jnp.int32)
        for a in range(blocks):
            value = value + total(place[a] == wide + b * TILE, packed[a])
        rest = value // TILE
        cut = pl.ds(b * TILE, TILE)
        plan[0:1, cut] = rest % (blocks * TILE)
        plan[1:2, cut] = value % TILE
        plan[2:3, cut] = rest // (blocks * TILE)
        upto = jnp.zeros((1, TILE), jnp.int32)
        here = jnp.zeros((1, TILE), jnp.int32)
        for a in range(blocks):
            upto = upto + total(row_down[a] <= wide)
            here = here + total(row_down[a] == wide)
        plan[3:4, cut] = jnp.where(here > 0, upto - 1, -1)


def product_kernel(
    count, rows_idx, cols_idx, tiles, probes, basis, factor, first_factor,
    own, gx, pairs, stage, xpair, sums, panel, near, mid, far,
    plan, table, mats, share, slices, grams, got_cols, got_rows, work, uppers, lowers,
    stage_sem, sa, ra, sb, rb, sc, rc, sd, rd, se, re, sf, rf, sg, rg,
    table_sem, sh, rh, si, ri, sj, rj,
):
    r, c = lax.axis_index("rows"), lax.axis_index("cols")
    y, z = r // SIDE, lax.rem(r, SIDE)
    x, q = c // 2, lax.rem(c, 2)

    def turn(v, off):
        return lax.rem(v + off + SIDE, SIDE)

    def yz(dim, off):
        return (turn(y, off), z) if dim == 0 else (y, turn(z, off))

    def row_peer(dim, off):
        yy, zz = yz(dim, off)
        return (yy * SIDE + zz, c)

    def x_peer(off):
        return (r, turn(x, off) * 2 + q)

    partner = (r, x * 2 + 1 - q)

    def load(i, slot):
        return pltpu.make_async_copy(tiles.at[pl.ds(i * STAGE, STAGE)], stage.at[slot], stage_sem.at[slot])

    for i in range(SLOTS):
        load(i, i).start()

    barrier = pltpu.get_barrier_semaphore()

    def col_mate(d):
        return (r, lax.rem(c + d, N_COLS))

    def row_mate(d):
        return (lax.rem(r + d, N_ROWS), c)

    for d in range(1, N_COLS):
        pl.semaphore_signal(barrier, inc=1, device_id=col_mate(d), device_id_type=MESH)
    for d in range(1, N_ROWS):
        pl.semaphore_signal(barrier, inc=1, device_id=row_mate(d), device_id_type=MESH)

    def turned(b, carry):
        block = jnp.transpose(probes[b])
        for j in range(PARTS):
            own[j, b] = block[j * WIDTH:(j + 1) * WIDTH]
            gx[j, y, z, b] = block[j * WIDTH:(j + 1) * WIDTH]
        return carry

    lax.fori_loop(0, OWN, turned, 0)
    pl.semaphore_wait(barrier, N_COLS - 1 + N_ROWS - 1)

    def remote(src, dst, send, recv, to):
        return pltpu.make_async_remote_copy(
            src_ref=src, dst_ref=dst, send_sem=send, recv_sem=recv, device_id=to, device_id_type=MESH)

    def step_of(s):
        return 1 if s == 0 else -1

    def copy_a(j, h, s):
        return remote(own.at[j, pl.ds(4 * h, 4)], gx.at[j, y, z, pl.ds(4 * h, 4)],
                      sa.at[j, h, s], ra.at[j, h, s], row_peer(1 - h, step_of(s)))

    def copy_b(j, h, s):
        yy, zz = yz(1 - h, -step_of(s))
        ref = gx.at[j, yy, zz, pl.ds(4 * h + 2 * s, 2)]
        return remote(ref, ref, sb.at[j, h, s], rb.at[j, h, s], row_peer(1 - h, step_of(s)))

    def copy_c(j, h, s):
        ref = gx.at[j, y, :, pl.ds(4 * h, 4)] if h == 0 else gx.at[j, :, z, pl.ds(4 * h, 4)]
        return remote(ref, ref, sc.at[j, h, s], rc.at[j, h, s], row_peer(h, step_of(s)))

    def copy_d(j, h, s):
        yy, zz = yz(h, -step_of(s))
        cut = pl.ds(4 * h + 2 * s, 2)
        ref = gx.at[j, yy, :, cut] if h == 0 else gx.at[j, :, zz, cut]
        return remote(ref, ref, sd.at[j, h, s], rd.at[j, h, s], row_peer(h, step_of(s)))

    ways = [(h, s) for h in (0, 1) for s in (0, 1)]

    def do_a(j):
        for h, s in ways:
            copy_a(j, h, s).start()

    def do_b(j):
        for h, s in ways:
            copy_a(j, h, s).wait_recv()
            copy_b(j, h, s).start()

    def do_c(j):
        for h in (0, 1):
            copy_b(j, h, 0).wait_recv()
            copy_b(j, h, 1).wait_recv()
            copy_c(j, h, 0).start()
            copy_c(j, h, 1).start()

    def do_d(j):
        for h, s in ways:
            copy_c(j, h, s).wait_recv()
            copy_d(j, h, s).start()

    def do_e(j):
        for h, s in ways:
            copy_d(j, h, s).wait_recv()

    def split(i, carry):
        slot = lax.rem(i, SLOTS)
        load(i, slot).wait()
        for k in range(STAGE):
            high, low = halves(jnp.transpose(stage[slot, k]))
            pairs[i * STAGE + k, 0:TILE] = high
            pairs[i * STAGE + k, TILE:2 * TILE] = low

        @pl.when(i + SLOTS < CAP // STAGE)
        def _():
            load(i + SLOTS, slot).start()

        return carry

    def spread(j):
        def one(g, carry):
            high, low = halves(gx[j, g // 32, lax.rem(g // 8, 4), lax.rem(g, 8)])
            xpair[g, 0:WIDTH, 0:TILE] = high
            xpair[g, 0:WIDTH, TILE:2 * TILE] = high
            xpair[g, WIDTH:2 * WIDTH, 0:TILE] = low
            xpair[g, WIDTH:2 * WIDTH, TILE:2 * TILE] = low
            return carry

        lax.fori_loop(0, N_ROWS * OWN, one, 0, unroll=8)

    def multiply(first, count, run):
        def group(g, run):
            for u in range(GROUP):
                t = first + g * GROUP + u
                both = jnp.dot(xpair[table[1, t]], pairs[table[0, t]], preferred_element_type=jnp.float32)
                run = run * table[2, t].astype(jnp.float32) + (both[:WIDTH] + both[WIDTH:])
                sums[t] = run
            return run

        return lax.fori_loop(0, count // GROUP, group, run)

    def collect(j):
        def one(i, carry):
            at = table[3, i]
            panel[j, i // 16, lax.rem(i // 8, 2), lax.rem(i, 8)] = jnp.where(
                at >= 0, sums[jnp.maximum(at, 0)], 0.0)
            return carry

        lax.fori_loop(0, PANEL, one, 0, unroll=8)

    def swap(j):
        return remote(panel.at[j, :, 1 - q], near.at[j], se.at[j], re.at[j], partner)

    def copy_f(j, s):
        return remote(panel.at[j, turn(x, 2), q, pl.ds(4 * s, 4)], mid.at[j, s],
                      sf.at[j, s], rf.at[j, s], x_peer(step_of(s)))

    def copy_g(j, s):
        return remote(panel.at[j, turn(x, step_of(s)), q], far.at[j, s],
                      sg.at[j, s], rg.at[j, s], x_peer(step_of(s)))

    def do_p(j):
        collect(j)
        swap(j).start()

    def do_q(j):
        swap(j).wait_recv()
        for off in (2, 1, -1, 0):
            at = turn(x, off)
            panel[j, at, q] = panel[j, at, q] + near[j, at]
            if off == 2:
                copy_f(j, 0).start()
                copy_f(j, 1).start()

    def do_r(j):
        for s in (0, 1):
            copy_f(j, s).wait_recv()
            at = turn(x, step_of(s))
            cut = pl.ds(4 * s, 4)
            panel[j, at, q, cut] = panel[j, at, q, cut] + mid[j, s]
            copy_g(j, s).start()

    def do_s(j):
        copy_g(j, 0).wait_recv()
        copy_g(j, 1).wait_recv()
        mats[0, :, j * WIDTH:(j + 1) * WIDTH, :] = panel[j, x, q] + (far[j, 0] + far[j, 1])

    steps = CAP // STAGE

    def some(lo, hi):
        lax.fori_loop(lo, hi, split, 0)

    for j in range(PARTS):
        do_a(j)
    sort_slots(count[0, 0], rows_idx, cols_idx, plan)
    to_scalars = pltpu.make_async_copy(plan, table, table_sem)
    to_scalars.start()
    some(0, 3)
    do_b(0)
    some(3, 6)
    do_b(1)
    some(6, 9)
    do_b(2)
    do_c(0)
    some(9, 14)
    do_b(3)
    do_c(1)
    some(14, 26)
    do_d(0)
    do_c(2)
    some(26, steps)
    to_scalars.wait()
    do_e(0)

    zero = jnp.zeros((WIDTH, TILE), jnp.float32)
    cuts = (0, 64, 160, 224, 320)

    def part(j, between):
        spread(j)
        run = zero
        for k in range(4):
            run = multiply(cuts[k], cuts[k + 1] - cuts[k], run)
            for act, i in between[k]:
                act(i)

    part(0, [[(do_d, 1), (do_c, 3)], [], [], [(do_p, 0)]])
    do_e(1)
    part(1, [[(do_q, 0)], [(do_d, 2)], [], [(do_r, 0), (do_p, 1)]])
    do_e(2)
    part(2, [[(do_d, 3)], [(do_q, 1), (do_s, 0)], [], [(do_r, 1), (do_p, 2)]])
    do_e(3)
    part(3, [[], [(do_q, 2), (do_s, 1)], [], [(do_r, 2), (do_p, 3)]])
    do_q(3)
    do_s(2)
    do_r(3)
    do_s(3)

    def copy_h(p, d):
        to = lax.rem(c + d, N_COLS)
        return remote(share.at[p, to], got_cols.at[p, d], sh.at[p, d], rh.at[p, d], col_mate(d))

    def copy_i(p, d):
        return remote(slices.at[p], got_rows.at[p, r], si.at[p, d], ri.at[p, d], row_mate(d))

    def copy_j(p, d):
        return remote(grams.at[p, c], grams.at[p, c], sj.at[p, d], rj.at[p, d], col_mate(d))

    def orthogonal(p, carry):
        total = jnp.zeros((TILE, TILE), jnp.float32)
        for b in range(OWN):
            block = mats[p, b]
            total = total + exact(block, block, 1, 1)
        share[p] = total.reshape(N_COLS, SLICE, TILE)
        for d in range(1, N_COLS):
            copy_h(p, d).start()
        for d in range(1, N_COLS):
            copy_h(p, d).wait_recv()
        part = share[p, c]
        for d in range(1, N_COLS):
            part = part + got_cols[p, d]
        slices[p] = part
        got_rows[p, r] = part
        for d in range(1, N_ROWS):
            copy_i(p, d).start()
        for d in range(1, N_ROWS):
            copy_i(p, d).wait_recv()
        part = got_rows[p, 0]
        for d in range(1, N_ROWS):
            part = part + got_rows[p, d]
        grams[p, c] = part
        for d in range(1, N_COLS):
            copy_j(p, d).start()
        for d in range(1, N_COLS):
            copy_j(p, d).wait_recv()
        triangles(grams[p].reshape(TILE, TILE) / NODES, uppers.at[p], lowers.at[p], work)
        lower = lowers[p]
        for b in range(OWN):
            mats[p + 1, b] = exact(lower, mats[p, b], 1, 0)
        for d in range(1, N_COLS):
            copy_h(p, d).wait_send()
            copy_j(p, d).wait_send()
        for d in range(1, N_ROWS):
            copy_i(p, d).wait_send()
        return carry

    lax.fori_loop(0, 2, orthogonal, 0)
    for b in range(OWN):
        basis[b] = jnp.transpose(mats[2, b])
    first_factor[...] = uppers[0]
    factor[...] = exact(uppers[1], uppers[0], 1, 0)
    for j in range(PARTS):
        for h, s in ways:
            for copy in (copy_a, copy_b, copy_c, copy_d):
                copy(j, h, s).wait_send()
        swap(j).wait_send()
        for s in (0, 1):
            copy_f(j, s).wait_send()
            copy_g(j, s).wait_send()


def product(tiles, rows_idx, cols_idx, count, probes):
    scalar = pl.BlockSpec(memory_space=pltpu.SMEM)
    vector = pl.BlockSpec(memory_space=pltpu.VMEM)
    f32, bf16 = jnp.float32, jnp.bfloat16
    piece = (OWN, WIDTH, TILE)
    square = (TILE, TILE)
    slab = (SLICE, TILE)
    return pl.pallas_call(
        product_kernel,
        out_shape=[
            jax.ShapeDtypeStruct((OWN,) + square, f32),
            jax.ShapeDtypeStruct(square, f32),
            jax.ShapeDtypeStruct(square, f32),
        ],
        in_specs=[scalar, vector, vector, pl.BlockSpec(memory_space=pl.ANY), vector],
        out_specs=[vector] * 3,
        scratch_shapes=[
            pltpu.VMEM((PARTS,) + piece, f32),
            pltpu.VMEM((PARTS, SIDE, SIDE) + piece, f32),
            pltpu.VMEM((CAP, 2 * TILE, TILE), bf16),
            pltpu.VMEM((SLOTS, STAGE, TILE, TILE), f32),
            pltpu.VMEM((N_ROWS * OWN, 2 * WIDTH, 2 * TILE), bf16),
            pltpu.VMEM((CAP, WIDTH, TILE), f32),
            pltpu.VMEM((PARTS, SIDE, 2) + piece, f32),
            pltpu.VMEM((PARTS, SIDE) + piece, f32),
            pltpu.VMEM((PARTS, 2, OWN // 2, WIDTH, TILE), f32),
            pltpu.VMEM((PARTS, 2) + piece, f32),
            pltpu.VMEM((8, 3 * TILE), jnp.int32),
            pltpu.SMEM((8, 3 * TILE), jnp.int32),
            pltpu.VMEM((3, OWN) + square, f32),
            pltpu.VMEM((2, N_COLS) + slab, f32),
            pltpu.VMEM((2,) + slab, f32),
            pltpu.VMEM((2, N_COLS) + slab, f32),
            pltpu.VMEM((2, N_COLS) + slab, f32),
            pltpu.VMEM((2, N_ROWS) + slab, f32),
            pltpu.VMEM((TILE, 2 * TILE), f32),
            pltpu.VMEM((2,) + square, f32),
            pltpu.VMEM((2,) + square, f32),
            DMA((SLOTS,)),
        ]
        + [DMA((PARTS, 2, 2))] * 8
        + [DMA((PARTS,))] * 2
        + [DMA((PARTS, 2))] * 4
        + [DMA(())]
        + [DMA((2, N_COLS))] * 2
        + [DMA((2, N_ROWS))] * 2
        + [DMA((2, N_COLS))] * 2,
        compiler_params=pltpu.CompilerParams(
            collective_id=2, has_side_effects=True, vmem_limit_bytes=60 * 2**20),
        name="node_basis",
    )(count, rows_idx, cols_idx, tiles, probes.reshape((OWN,) + square))


def shards(tile_values, tile_rows, tile_cols, tile_count, probes):
    basis, factor, first_factor = product(
        tile_values[0, 0], tile_rows[0], tile_cols[0], tile_count, probes)
    return basis.reshape(probes.shape), factor, first_factor


def solution(mesh):
    placed = (
        P("rows", "cols", None, None, None),
        P("rows", "cols", None),
        P("rows", "cols", None),
        P("rows", "cols"),
        P(("rows", "cols"), None),
    )
    return jax.shard_map(
        shards,
        mesh=mesh,
        in_specs=placed,
        out_specs=(P(("rows", "cols"), None), P(), P()),
        check_vma=False,
    )
```

```python
import jax
import jax.numpy as jnp
from jax import lax
from jax.experimental import pallas as pl
from jax.experimental.pallas import tpu as pltpu
from jax.sharding import PartitionSpec as P

SIDE = 4
N_ROWS = SIDE * SIDE
N_COLS = 8
TILE = 128
CAP = 320
OWN = 8
PANEL = OWN * N_COLS
PARTS = 4
WIDTH = TILE // PARTS
GROUP = 32
STAGE = 8
STRIP = 16
SLICE = TILE // N_COLS
SPREAD = 1.5
NODES = OWN * TILE * N_ROWS * N_COLS
SLOTS = 8
MESH = pl.DeviceIdType.MESH
DMA = pltpu.SemaphoreType.DMA


def halves(value):
    high = value.astype(jnp.bfloat16)
    low = (value - high.astype(jnp.float32)).astype(jnp.bfloat16)
    return high, low


def exact(left, right, at, to):
    return lax.dot_general(
        left, right, (((at,), (to,)), ((), ())), precision=lax.Precision.HIGHEST,
        preferred_element_type=jnp.float32)


def triangles(gram, upper, inverse, work):
    rows = lax.broadcasted_iota(jnp.int32, (TILE, TILE), 0)
    cols = lax.broadcasted_iota(jnp.int32, (TILE, TILE), 1)
    work[:, 0:TILE] = gram
    work[:, TILE:2 * TILE] = jnp.where(rows == cols, 1.0, 0.0)
    shape = (STRIP, TILE)
    place = lax.broadcasted_iota(jnp.int32, shape, 0)
    for lo in range(0, TILE, STRIP):
        hi = lo + STRIP
        strip = work[lo:hi, 0:TILE]
        turned = work[lo:hi, TILE:2 * TILE]
        columns = [jnp.broadcast_to(strip[:, lo + j:lo + j + 1], shape) for j in range(STRIP)]
        for k in range(STRIP):
            scale = lax.rsqrt(jnp.broadcast_to(columns[k][k:k + 1], shape))
            weight = columns[k] * scale
            for j in range(k + 1, STRIP):
                columns[j] = columns[j] - weight * jnp.broadcast_to(weight[j:j + 1], shape)
            pivot = jnp.broadcast_to(strip[k:k + 1], shape) * scale
            other = jnp.broadcast_to(turned[k:k + 1], shape) * scale
            weight = jnp.where(place > k, weight, 0.0)
            strip = jnp.where(place == k, pivot, strip - weight * pivot)
            turned = jnp.where(place == k, other, turned - weight * other)
        strip = jnp.where(cols[lo:hi] >= rows[lo:hi], strip, 0.0)
        upper[lo:hi, :] = strip
        inverse[lo:hi, :] = turned
        if hi < TILE:
            change = exact(strip, jnp.concatenate([strip, turned], axis=1), 0, 0)
            work[hi:, :] = work[hi:, :] - change[hi:, :]


def sort_slots(count, rows_idx, cols_idx, plan):
    blocks = CAP // TILE + 1
    square = (TILE, TILE)
    lane = lax.broadcasted_iota(jnp.int32, (1, TILE), 1)
    high = lax.broadcasted_iota(jnp.int32, square, 0)
    wide = lax.broadcasted_iota(jnp.int32, square, 1)

    def block(ref, b):
        width = min(TILE, CAP - b * TILE)
        value = ref[:, b * TILE:b * TILE + width]
        if width < TILE:
            value = jnp.concatenate([value, jnp.zeros((1, TILE - width), jnp.int32)], axis=1)
        return value

    def down(value):
        return jnp.transpose(jnp.broadcast_to(value, square))

    def total(mask, value=1):
        return jnp.sum(jnp.where(mask, value, 0), axis=0, keepdims=True)

    slot = [lane + b * TILE for b in range(blocks)]
    row = [jnp.where(slot[b] < count, block(rows_idx, b), PANEL) for b in range(blocks)]
    row_down = [down(v) for v in row]
    place, packed = [], []
    for b in range(blocks):
        rank = jnp.zeros((1, TILE), jnp.int32)
        before = jnp.zeros((1, TILE), jnp.int32)
        for a in range(blocks):
            same = row_down[a] == row[b]
            if a == b:
                same = jnp.logical_and(same, high < wide)
            earlier = row_down[a] < row[b]
            if a <= b:
                earlier = jnp.logical_or(earlier, same)
                before = before + total(same)
            rank = rank + total(earlier)
        place.append(down(rank))
        goes_on = jnp.where(before > 0, 1, 0)
        packed.append(down((goes_on * blocks * TILE + slot[b]) * TILE + block(cols_idx, b)))
    for b in range(blocks):
        value = jnp.zeros((1, TILE), jnp.int32)
        for a in range(blocks):
            value = value + total(place[a] == wide + b * TILE, packed[a])
        rest = value // TILE
        cut = pl.ds(b * TILE, TILE)
        plan[0:1, cut] = rest % (blocks * TILE)
        plan[1:2, cut] = value % TILE
        plan[2:3, cut] = rest // (blocks * TILE)
        upto = jnp.zeros((1, TILE), jnp.int32)
        here = jnp.zeros((1, TILE), jnp.int32)
        for a in range(blocks):
            upto = upto + total(row_down[a] <= wide)
            here = here + total(row_down[a] == wide)
        plan[3:4, cut] = jnp.where(here > 0, upto - 1, -1)


def product_kernel(
    count, rows_idx, cols_idx, tiles, probes, plain, scaled, upper, inverse, health,
    own, gx, pairs, stage, xpair, sums, panel, near, mid, far,
    plan, table, mats, share, slices, grams, got_cols, got_rows, work, uppers, lowers,
    stage_sem, sa, ra, sb, rb, sc, rc, sd, rd, se, re, sf, rf, sg, rg,
    table_sem, sh, rh, si, ri, sj, rj,
):
    r, c = lax.axis_index("rows"), lax.axis_index("cols")
    y, z = r // SIDE, lax.rem(r, SIDE)
    x, q = c // 2, lax.rem(c, 2)

    def turn(v, off):
        return lax.rem(v + off + SIDE, SIDE)

    def yz(dim, off):
        return (turn(y, off), z) if dim == 0 else (y, turn(z, off))

    def row_peer(dim, off):
        yy, zz = yz(dim, off)
        return (yy * SIDE + zz, c)

    def x_peer(off):
        return (r, turn(x, off) * 2 + q)

    partner = (r, x * 2 + 1 - q)

    def load(i, slot):
        return pltpu.make_async_copy(tiles.at[pl.ds(i * STAGE, STAGE)], stage.at[slot], stage_sem.at[slot])

    for i in range(SLOTS):
        load(i, i).start()

    barrier = pltpu.get_barrier_semaphore()

    def col_mate(d):
        return (r, lax.rem(c + d, N_COLS))

    def row_mate(d):
        return (lax.rem(r + d, N_ROWS), c)

    for d in range(1, N_COLS):
        pl.semaphore_signal(barrier, inc=1, device_id=col_mate(d), device_id_type=MESH)
    for d in range(1, N_ROWS):
        pl.semaphore_signal(barrier, inc=1, device_id=row_mate(d), device_id_type=MESH)

    def turned(b, carry):
        block = jnp.transpose(probes[b])
        mats[0, b] = block
        for j in range(PARTS):
            own[j, b] = block[j * WIDTH:(j + 1) * WIDTH]
            gx[j, y, z, b] = block[j * WIDTH:(j + 1) * WIDTH]
        return carry

    lax.fori_loop(0, OWN, turned, 0)
    pl.semaphore_wait(barrier, N_COLS - 1 + N_ROWS - 1)

    def remote(src, dst, send, recv, to):
        return pltpu.make_async_remote_copy(
            src_ref=src, dst_ref=dst, send_sem=send, recv_sem=recv, device_id=to, device_id_type=MESH)

    def step_of(s):
        return 1 if s == 0 else -1

    def half(h, s, f):
        return pl.ds(4 * h + 2 * (s if f == 0 else 1 - s), 2)

    def copy_a(j, h, s, f):
        cut = half(h, s, f)
        return remote(own.at[j, cut], gx.at[j, y, z, cut],
                      sa.at[j, h, s, f], ra.at[j, h, s, f], row_peer(1 - h, step_of(s)))

    def copy_b(j, h, s):
        yy, zz = yz(1 - h, -step_of(s))
        ref = gx.at[j, yy, zz, half(h, s, 0)]
        return remote(ref, ref, sb.at[j, h, s], rb.at[j, h, s], row_peer(1 - h, step_of(s)))

    def copy_c(j, h, s, f):
        cut = half(h, s, f)
        ref = gx.at[j, y, :, cut] if h == 0 else gx.at[j, :, z, cut]
        return remote(ref, ref, sc.at[j, h, s, f], rc.at[j, h, s, f], row_peer(h, step_of(s)))

    def copy_d(j, h, s):
        yy, zz = yz(h, -step_of(s))
        cut = half(h, s, 0)
        ref = gx.at[j, yy, :, cut] if h == 0 else gx.at[j, :, zz, cut]
        return remote(ref, ref, sd.at[j, h, s], rd.at[j, h, s], row_peer(h, step_of(s)))

    ways = [(h, s) for h in (0, 1) for s in (0, 1)]

    def do_a(j):
        for f in (0, 1):
            for h, s in ways:
                copy_a(j, h, s, f).start()

    def do_b(j):
        for h, s in ways:
            copy_a(j, h, s, 0).wait_recv()
            copy_b(j, h, s).start()

    def do_c(j):
        for h, s in ways:
            copy_a(j, h, s, 1).wait_recv()
        for h, s in ways:
            copy_b(j, h, s).wait_recv()
        for h, s in ways:
            copy_c(j, h, s, 0).start()

    def do_cc(j):
        for h, s in ways:
            copy_c(j, h, s, 1).start()

    def do_d(j):
        for h, s in ways:
            copy_c(j, h, s, 0).wait_recv()
            copy_d(j, h, s).start()

    def do_e(j):
        for h, s in ways:
            copy_c(j, h, s, 1).wait_recv()
            copy_d(j, h, s).wait_recv()

    def split(i, carry):
        slot = lax.rem(i, SLOTS)
        load(i, slot).wait()
        for k in range(STAGE):
            high, low = halves(jnp.transpose(stage[slot, k]))
            pairs[i * STAGE + k, 0:TILE] = high
            pairs[i * STAGE + k, TILE:2 * TILE] = low

        @pl.when(i + SLOTS < CAP // STAGE)
        def _():
            load(i + SLOTS, slot).start()

        return carry

    def spread(j):
        def one(g, carry):
            high, low = halves(gx[j, g // 32, lax.rem(g // 8, 4), lax.rem(g, 8)])
            xpair[g, 0:WIDTH, 0:TILE] = high
            xpair[g, 0:WIDTH, TILE:2 * TILE] = high
            xpair[g, WIDTH:2 * WIDTH, 0:TILE] = low
            xpair[g, WIDTH:2 * WIDTH, TILE:2 * TILE] = low
            return carry

        lax.fori_loop(0, N_ROWS * OWN, one, 0, unroll=8)

    def multiply(first, count, run):
        def group(g, run):
            for u in range(GROUP):
                t = first + g * GROUP + u
                both = jnp.dot(xpair[table[1, t]], pairs[table[0, t]], preferred_element_type=jnp.float32)
                run = run * table[2, t].astype(jnp.float32) + (both[:WIDTH] + both[WIDTH:])
                sums[t] = run
            return run

        return lax.fori_loop(0, count // GROUP, group, run)

    def collect(j):
        def one(i, carry):
            at = table[3, i]
            panel[j, i // 16, lax.rem(i // 8, 2), lax.rem(i, 8)] = jnp.where(
                at >= 0, sums[jnp.maximum(at, 0)], 0.0)
            return carry

        lax.fori_loop(0, PANEL, one, 0, unroll=8)

    def swap(j, off):
        at = turn(x, off)
        i = off % SIDE
        return remote(panel.at[j, at, 1 - q], near.at[j, at], se.at[j, i], re.at[j, i], partner)

    def copy_f(j, s):
        return remote(panel.at[j, turn(x, 2), q, pl.ds(4 * s, 4)], mid.at[j, s],
                      sf.at[j, s], rf.at[j, s], x_peer(step_of(s)))

    def copy_g(j, s, f):
        cut = pl.ds(4 * (1 - s if f == 0 else s), 4)
        return remote(panel.at[j, turn(x, step_of(s)), q, cut], far.at[j, s, cut],
                      sg.at[j, s, f], rg.at[j, s, f], x_peer(step_of(s)))

    offs = (2, 1, -1, 0)

    def do_p(j):
        collect(j)
        for off in offs:
            swap(j, off).start()

    def do_q(j):
        for off in offs:
            swap(j, off).wait_recv()
            at = turn(x, off)
            panel[j, at, q] = panel[j, at, q] + near[j, at]
            if off == 2:
                copy_f(j, 0).start()
                copy_f(j, 1).start()
            elif off != 0:
                copy_g(j, 0 if off == 1 else 1, 0).start()

    def do_r(j):
        for s in (0, 1):
            copy_f(j, s).wait_recv()
            at = turn(x, step_of(s))
            cut = pl.ds(4 * s, 4)
            panel[j, at, q, cut] = panel[j, at, q, cut] + mid[j, s]
            copy_g(j, s, 1).start()

    def do_s(j):
        for s in (0, 1):
            for f in (0, 1):
                copy_g(j, s, f).wait_recv()
        mats[1, :, j * WIDTH:(j + 1) * WIDTH, :] = panel[j, x, q] + (far[j, 0] + far[j, 1])

    def copy_h(p, d):
        to = lax.rem(c + d, N_COLS)
        return remote(share.at[p, to], got_cols.at[p, d], sh.at[p, d], rh.at[p, d], col_mate(d))

    def copy_i(p, d):
        return remote(slices.at[p], got_rows.at[p, r], si.at[p, d], ri.at[p, d], row_mate(d))

    def copy_j(p, d):
        return remote(grams.at[p, c], grams.at[p, c], sj.at[p, d], rj.at[p, d], col_mate(d))

    def sum_start(p, at):
        total = jnp.zeros((TILE, TILE), jnp.float32)
        for b in range(OWN):
            block = mats[at, b]
            total = total + exact(block, block, 1, 1)
        share[p] = total.reshape(N_COLS, SLICE, TILE)
        for d in range(1, N_COLS):
            copy_h(p, d).start()

    def sum_rows(p):
        for d in range(1, N_COLS):
            copy_h(p, d).wait_recv()
        part = share[p, c]
        for d in range(1, N_COLS):
            part = part + got_cols[p, d]
        slices[p] = part
        got_rows[p, r] = part
        for d in range(1, N_ROWS):
            copy_i(p, d).start()

    def sum_cols(p):
        for d in range(1, N_ROWS):
            copy_i(p, d).wait_recv()
        part = got_rows[p, 0]
        for d in range(1, N_ROWS):
            part = part + got_rows[p, d]
        grams[p, c] = part
        for d in range(1, N_COLS):
            copy_j(p, d).start()

    def sum_end(p):
        for d in range(1, N_COLS):
            copy_j(p, d).wait_recv()
        triangles(grams[p].reshape(TILE, TILE) / NODES, uppers.at[p], lowers.at[p], work)

    steps = CAP // STAGE

    def some(lo, hi):
        lax.fori_loop(lo, hi, split, 0)

    for j in range(PARTS):
        do_a(j)
    sum_start(0, 0)
    sort_slots(count[0, 0], rows_idx, cols_idx, plan)
    to_scalars = pltpu.make_async_copy(plan, table, table_sem)
    to_scalars.start()
    do_b(0)
    do_b(1)
    sum_rows(0)
    some(0, 4)
    do_b(2)
    do_b(3)
    do_c(0)
    do_cc(0)
    do_c(1)
    some(4, 16)
    sum_cols(0)
    some(16, 26)
    do_d(0)
    do_cc(1)
    do_c(2)
    some(26, steps)
    to_scalars.wait()
    sum_end(0)
    do_d(1)
    do_cc(2)
    do_c(3)
    do_e(0)

    zero = jnp.zeros((WIDTH, TILE), jnp.float32)
    cuts = (0, 64, 160, 224, 320)

    def part(j, between):
        spread(j)
        run = zero
        for k in range(4):
            run = multiply(cuts[k], cuts[k + 1] - cuts[k], run)
            for act, i in between[k]:
                act(i)

    part(0, [[], [], [], [(do_p, 0), (do_d, 2), (do_cc, 3)]])
    do_e(1)
    part(1, [[], [(do_q, 0)], [], [(do_r, 0), (do_d, 3), (do_p, 1)]])
    do_e(2)
    part(2, [[], [(do_q, 1), (do_s, 0)], [], [(do_r, 1), (do_p, 2)]])
    do_e(3)
    part(3, [[], [(do_q, 2), (do_s, 1)], [], [(do_r, 2), (do_p, 3)]])
    do_q(3)
    do_s(2)
    do_r(3)
    do_s(3)

    lower = lowers[0]
    for b in range(OWN):
        mats[2, b] = exact(lower, mats[1, b], 1, 0)
    sum_start(1, 2)
    sum_rows(1)
    sum_cols(1)
    sum_end(1)
    plain[...] = mats[1]
    scaled[...] = mats[2]
    upper[...] = uppers[...]
    inverse[...] = lowers[1]
    spread_of = jnp.sum(jnp.square(uppers[1]), keepdims=True) * jnp.sum(jnp.square(lowers[1]), keepdims=True)
    health[...] = jnp.broadcast_to(spread_of / (TILE * TILE), (8, TILE))

    for j in range(PARTS):
        for h, s in ways:
            for f in (0, 1):
                copy_a(j, h, s, f).wait_send()
                copy_c(j, h, s, f).wait_send()
            copy_b(j, h, s).wait_send()
            copy_d(j, h, s).wait_send()
        for off in offs:
            swap(j, off).wait_send()
        for s in (0, 1):
            copy_f(j, s).wait_send()
            copy_g(j, s, 0).wait_send()
            copy_g(j, s, 1).wait_send()
    for p in (0, 1):
        for d in range(1, N_COLS):
            copy_h(p, d).wait_send()
            copy_j(p, d).wait_send()
        for d in range(1, N_ROWS):
            copy_i(p, d).wait_send()


def finish_kernel(scaled, upper, inverse, basis, factor, first_factor):
    for b in range(OWN):
        basis[b] = jnp.transpose(exact(inverse[...], scaled[b], 1, 0))
    whole = exact(upper[1], upper[0], 1, 0)
    factor[...] = whole
    first_factor[...] = whole


def product(tiles, rows_idx, cols_idx, count, probes):
    scalar = pl.BlockSpec(memory_space=pltpu.SMEM)
    vector = pl.BlockSpec(memory_space=pltpu.VMEM)
    f32, bf16 = jnp.float32, jnp.bfloat16
    piece = (OWN, WIDTH, TILE)
    square = (TILE, TILE)
    slab = (SLICE, TILE)
    return pl.pallas_call(
        product_kernel,
        out_shape=[
            jax.ShapeDtypeStruct((OWN,) + square, f32),
            jax.ShapeDtypeStruct((OWN,) + square, f32),
            jax.ShapeDtypeStruct((2,) + square, f32),
            jax.ShapeDtypeStruct(square, f32),
            jax.ShapeDtypeStruct((8, TILE), f32),
        ],
        in_specs=[scalar, vector, vector, pl.BlockSpec(memory_space=pl.ANY), vector],
        out_specs=[vector] * 5,
        scratch_shapes=[
            pltpu.VMEM((PARTS,) + piece, f32),
            pltpu.VMEM((PARTS, SIDE, SIDE) + piece, f32),
            pltpu.VMEM((CAP, 2 * TILE, TILE), bf16),
            pltpu.VMEM((SLOTS, STAGE, TILE, TILE), f32),
            pltpu.VMEM((N_ROWS * OWN, 2 * WIDTH, 2 * TILE), bf16),
            pltpu.VMEM((CAP, WIDTH, TILE), f32),
            pltpu.VMEM((PARTS, SIDE, 2) + piece, f32),
            pltpu.VMEM((PARTS, SIDE) + piece, f32),
            pltpu.VMEM((PARTS, 2, OWN // 2, WIDTH, TILE), f32),
            pltpu.VMEM((PARTS, 2) + piece, f32),
            pltpu.VMEM((8, 3 * TILE), jnp.int32),
            pltpu.SMEM((8, 3 * TILE), jnp.int32),
            pltpu.VMEM((3, OWN) + square, f32),
            pltpu.VMEM((2, N_COLS) + slab, f32),
            pltpu.VMEM((2,) + slab, f32),
            pltpu.VMEM((2, N_COLS) + slab, f32),
            pltpu.VMEM((2, N_COLS) + slab, f32),
            pltpu.VMEM((2, N_ROWS) + slab, f32),
            pltpu.VMEM((TILE, 2 * TILE), f32),
            pltpu.VMEM((2,) + square, f32),
            pltpu.VMEM((2,) + square, f32),
            DMA((SLOTS,)),
        ]
        + [DMA((PARTS, 2, 2, 2))] * 2
        + [DMA((PARTS, 2, 2))] * 2
        + [DMA((PARTS, 2, 2, 2))] * 2
        + [DMA((PARTS, 2, 2))] * 2
        + [DMA((PARTS, SIDE))] * 2
        + [DMA((PARTS, 2))] * 2
        + [DMA((PARTS, 2, 2))] * 2
        + [DMA(())]
        + [DMA((2, N_COLS))] * 2
        + [DMA((2, N_ROWS))] * 2
        + [DMA((2, N_COLS))] * 2,
        compiler_params=pltpu.CompilerParams(
            collective_id=2, has_side_effects=True, vmem_limit_bytes=60 * 2**20),
        name="node_basis",
    )(count, rows_idx, cols_idx, tiles, probes.reshape((OWN,) + square))


def finish(scaled, upper, inverse):
    vector = pl.BlockSpec(memory_space=pltpu.VMEM)
    square = jax.ShapeDtypeStruct((TILE, TILE), jnp.float32)
    return pl.pallas_call(
        finish_kernel,
        out_shape=[jax.ShapeDtypeStruct(scaled.shape, jnp.float32), square, square],
        in_specs=[vector] * 3,
        out_specs=[vector] * 3,
        compiler_params=pltpu.CompilerParams(vmem_limit_bytes=16 * 2**20),
        name="finish",
    )(scaled, upper, inverse)


def signal_all(sem, r, c):
    def cols_peer(d, carry):
        pl.semaphore_signal(sem, inc=1, device_id=(r, lax.rem(c + d, N_COLS)), device_id_type=MESH)
        return carry

    def rows_peer(d, carry):
        pl.semaphore_signal(sem, inc=1, device_id=(lax.rem(r + d, N_ROWS), c), device_id_type=MESH)
        return carry

    lax.fori_loop(1, N_COLS, cols_peer, 0)
    lax.fori_loop(1, N_ROWS, rows_peer, 0)


def sum_kernel(g_ref, out_ref, part, got_a, got_b, send_a, recv_a, send_b, recv_b, send_c, recv_c):
    r, c = lax.axis_index("rows"), lax.axis_index("cols")
    barrier = pltpu.get_barrier_semaphore()
    signal_all(barrier, r, c)
    pl.semaphore_wait(barrier, N_COLS - 1 + N_ROWS - 1)

    def copy_a(d):
        to = lax.rem(c + d, N_COLS)
        return pltpu.make_async_remote_copy(
            src_ref=g_ref.at[to], dst_ref=got_a.at[d], send_sem=send_a.at[d], recv_sem=recv_a.at[d],
            device_id=(r, to), device_id_type=MESH)

    def copy_b(d):
        return pltpu.make_async_remote_copy(
            src_ref=part, dst_ref=got_b.at[r], send_sem=send_b.at[d], recv_sem=recv_b.at[d],
            device_id=(lax.rem(r + d, N_ROWS), c), device_id_type=MESH)

    def copy_c(d):
        return pltpu.make_async_remote_copy(
            src_ref=out_ref.at[c], dst_ref=out_ref.at[c], send_sem=send_c.at[d], recv_sem=recv_c.at[d],
            device_id=(r, lax.rem(c + d, N_COLS)), device_id_type=MESH)

    def each(copy, n, act):
        def step(d, carry):
            getattr(copy(d), act)()
            return carry

        lax.fori_loop(1, n, step, 0)

    each(copy_a, N_COLS, "start")
    each(copy_a, N_COLS, "wait_recv")
    total = g_ref[c]
    for d in range(1, N_COLS):
        total = total + got_a[d]
    part[...] = total
    got_b[r] = total
    each(copy_b, N_ROWS, "start")
    each(copy_a, N_COLS, "wait_send")
    each(copy_b, N_ROWS, "wait_recv")
    total = got_b[0]
    for d in range(1, N_ROWS):
        total = total + got_b[d]
    out_ref[c] = total
    each(copy_c, N_COLS, "start")
    each(copy_b, N_ROWS, "wait_send")
    each(copy_c, N_COLS, "wait")


def sum_everywhere(matrix, ident):
    size = matrix.shape[0]
    rows = size // N_COLS
    piece = (rows, size)
    out = pl.pallas_call(
        sum_kernel,
        out_shape=jax.ShapeDtypeStruct((N_COLS,) + piece, jnp.float32),
        in_specs=[pl.BlockSpec(memory_space=pltpu.VMEM)],
        out_specs=pl.BlockSpec(memory_space=pltpu.VMEM),
        scratch_shapes=[
            pltpu.VMEM(piece, jnp.float32),
            pltpu.VMEM((N_COLS,) + piece, jnp.float32),
            pltpu.VMEM((N_ROWS,) + piece, jnp.float32),
            DMA((N_COLS,)), DMA((N_COLS,)), DMA((N_ROWS,)), DMA((N_ROWS,)), DMA((N_COLS,)), DMA((N_COLS,)),
        ],
        compiler_params=pltpu.CompilerParams(collective_id=ident, has_side_effects=True),
        name="sum_everywhere",
    )(matrix.reshape((N_COLS,) + piece))
    return out.reshape(size, size)


def two_passes(matrix):
    def normal(value):
        gram = jnp.einsum("rk,rl->kl", value, value, precision=lax.Precision.HIGHEST)
        lower = jnp.linalg.cholesky(sum_everywhere(gram, 1) / NODES)
        inverse = jax.scipy.linalg.solve_triangular(
            lower, jnp.eye(TILE, dtype=jnp.float32), lower=True)
        return jnp.dot(value, inverse.T, precision=lax.Precision.HIGHEST), lower

    first, lower = normal(matrix)
    basis, lower_next = normal(first)
    return basis, jnp.dot(lower_next.T, lower.T, precision=lax.Precision.HIGHEST), lower.T


def shards(tile_values, tile_rows, tile_cols, tile_count, probes):
    plain, scaled, upper, inverse, health = product(
        tile_values[0, 0], tile_rows[0], tile_cols[0], tile_count, probes)

    def well():
        basis, factor, first_factor = finish(scaled, upper, inverse)
        return basis.reshape(probes.shape), factor, first_factor

    def ill():
        return two_passes(jnp.swapaxes(plain, 1, 2).reshape(probes.shape))

    return lax.cond(health[0, 0] < SPREAD, well, ill)


def solution(mesh):
    placed = (
        P("rows", "cols", None, None, None),
        P("rows", "cols", None),
        P("rows", "cols", None),
        P("rows", "cols"),
        P(("rows", "cols"), None),
    )
    return jax.shard_map(
        shards,
        mesh=mesh,
        in_specs=placed,
        out_specs=(P(("rows", "cols"), None), P(), P()),
        check_vma=False,
    )
```

```python
import jax
import jax.numpy as jnp
from jax import lax
from jax.experimental import pallas as pl
from jax.experimental.pallas import tpu as pltpu
from jax.sharding import PartitionSpec as P

SIDE = 4
N_ROWS = SIDE * SIDE
N_COLS = 8
TILE = 128
CAP = 320
OWN = 8
PANEL = OWN * N_COLS
PARTS = 4
WIDTH = TILE // PARTS
GROUP = 40
STAGE = 8
STRIP = 16
SLICE = TILE // N_COLS
SPREAD = 1.5
NODES = OWN * TILE * N_ROWS * N_COLS
SLOTS = 8
MESH = pl.DeviceIdType.MESH
DMA = pltpu.SemaphoreType.DMA


def halves(value):
    high = value.astype(jnp.bfloat16)
    low = (value - high.astype(jnp.float32)).astype(jnp.bfloat16)
    return high, low


def exact(left, right, at, to):
    return lax.dot_general(
        left, right, (((at,), (to,)), ((), ())), precision=lax.Precision.HIGHEST,
        preferred_element_type=jnp.float32)


def triangles(gram, upper, inverse, work):
    rows = lax.broadcasted_iota(jnp.int32, (TILE, TILE), 0)
    cols = lax.broadcasted_iota(jnp.int32, (TILE, TILE), 1)
    work[:, 0:TILE] = gram
    work[:, TILE:2 * TILE] = jnp.where(rows == cols, 1.0, 0.0)
    shape = (STRIP, TILE)
    place = lax.broadcasted_iota(jnp.int32, shape, 0)
    for lo in range(0, TILE, STRIP):
        hi = lo + STRIP
        strip = work[lo:hi, 0:TILE]
        turned = work[lo:hi, TILE:2 * TILE]
        columns = [jnp.broadcast_to(strip[:, lo + j:lo + j + 1], shape) for j in range(STRIP)]
        for k in range(STRIP):
            scale = lax.rsqrt(jnp.broadcast_to(columns[k][k:k + 1], shape))
            weight = columns[k] * scale
            for j in range(k + 1, STRIP):
                columns[j] = columns[j] - weight * jnp.broadcast_to(weight[j:j + 1], shape)
            pivot = jnp.broadcast_to(strip[k:k + 1], shape) * scale
            other = jnp.broadcast_to(turned[k:k + 1], shape) * scale
            weight = jnp.where(place > k, weight, 0.0)
            strip = jnp.where(place == k, pivot, strip - weight * pivot)
            turned = jnp.where(place == k, other, turned - weight * other)
        strip = jnp.where(cols[lo:hi] >= rows[lo:hi], strip, 0.0)
        upper[lo:hi, :] = strip
        inverse[lo:hi, :] = turned
        if hi < TILE:
            change = exact(strip, jnp.concatenate([strip, turned], axis=1), 0, 0)
            work[hi:, :] = work[hi:, :] - change[hi:, :]


def sort_slots(count, rows_idx, cols_idx, plan):
    blocks = CAP // TILE + 1
    square = (TILE, TILE)
    lane = lax.broadcasted_iota(jnp.int32, (1, TILE), 1)
    high = lax.broadcasted_iota(jnp.int32, square, 0)
    wide = lax.broadcasted_iota(jnp.int32, square, 1)

    def block(ref, b):
        width = min(TILE, CAP - b * TILE)
        value = ref[:, b * TILE:b * TILE + width]
        if width < TILE:
            value = jnp.concatenate([value, jnp.zeros((1, TILE - width), jnp.int32)], axis=1)
        return value

    def down(value):
        return jnp.transpose(jnp.broadcast_to(value, square))

    def total(mask, value=1):
        return jnp.sum(jnp.where(mask, value, 0), axis=0, keepdims=True)

    slot = [lane + b * TILE for b in range(blocks)]
    row = [jnp.where(slot[b] < count, block(rows_idx, b), PANEL) for b in range(blocks)]
    row_down = [down(v) for v in row]
    place, packed = [], []
    for b in range(blocks):
        rank = jnp.zeros((1, TILE), jnp.int32)
        before = jnp.zeros((1, TILE), jnp.int32)
        for a in range(blocks):
            same = row_down[a] == row[b]
            if a == b:
                same = jnp.logical_and(same, high < wide)
            earlier = row_down[a] < row[b]
            if a <= b:
                earlier = jnp.logical_or(earlier, same)
                before = before + total(same)
            rank = rank + total(earlier)
        place.append(down(rank))
        goes_on = jnp.where(before > 0, 1, 0)
        packed.append(down((goes_on * blocks * TILE + slot[b]) * TILE + block(cols_idx, b)))
    for b in range(blocks):
        value = jnp.zeros((1, TILE), jnp.int32)
        for a in range(blocks):
            value = value + total(place[a] == wide + b * TILE, packed[a])
        rest = value // TILE
        cut = pl.ds(b * TILE, TILE)
        plan[0:1, cut] = rest % (blocks * TILE)
        plan[1:2, cut] = value % TILE
        plan[2:3, cut] = rest // (blocks * TILE)
        upto = jnp.zeros((1, TILE), jnp.int32)
        here = jnp.zeros((1, TILE), jnp.int32)
        for a in range(blocks):
            upto = upto + total(row_down[a] <= wide)
            here = here + total(row_down[a] == wide)
        plan[3:4, cut] = jnp.where(here > 0, upto - 1, -1)


def product_kernel(
    count_in, rows_in, cols_in, tiles, probes_in, plain, scaled, upper, inverse, health,
    count, rows_idx, cols_idx, probes, own, gx, pairs, stage, xpair, sums, panel, near, mid, far,
    plan, table, mats, share, slices, grams, got_cols, got_rows, work, uppers, lowers,
    stage_sem, sa, ra, sb, rb, sc, rc, sd, rd, se, re, sf, rf, sg, rg,
    table_sem, in_sem, out_sem, sh, rh, si, ri, sj, rj,
):
    r, c = lax.axis_index("rows"), lax.axis_index("cols")
    y, z = r // SIDE, lax.rem(r, SIDE)
    x, q = c // 2, lax.rem(c, 2)

    def turn(v, off):
        return lax.rem(v + off + SIDE, SIDE)

    def yz(dim, off):
        return (turn(y, off), z) if dim == 0 else (y, turn(z, off))

    def row_peer(dim, off):
        yy, zz = yz(dim, off)
        return (yy * SIDE + zz, c)

    def x_peer(off):
        return (r, turn(x, off) * 2 + q)

    partner = (r, x * 2 + 1 - q)

    def load(i, slot):
        return pltpu.make_async_copy(tiles.at[pl.ds(i * STAGE, STAGE)], stage.at[slot], stage_sem.at[slot])

    fetch = [
        pltpu.make_async_copy(src, dst, in_sem.at[i])
        for i, (src, dst) in enumerate(
            [(probes_in, probes), (rows_in, rows_idx), (cols_in, cols_idx), (count_in, count)])
    ]
    for copy in fetch:
        copy.start()

    barrier = pltpu.get_barrier_semaphore()

    def col_mate(d):
        return (r, lax.rem(c + d, N_COLS))

    def row_mate(d):
        return (lax.rem(r + d, N_ROWS), c)

    for d in range(1, N_COLS):
        pl.semaphore_signal(barrier, inc=1, device_id=col_mate(d), device_id_type=MESH)
    for d in range(1, N_ROWS):
        pl.semaphore_signal(barrier, inc=1, device_id=row_mate(d), device_id_type=MESH)

    for i in range(SLOTS):
        load(i, i).start()

    def turned(b, carry):
        block = jnp.transpose(probes[b])
        mats[0, b] = block
        for j in range(PARTS):
            own[j, b] = block[j * WIDTH:(j + 1) * WIDTH]
            gx[j, y, z, b] = block[j * WIDTH:(j + 1) * WIDTH]
        return carry

    fetch[0].wait()
    lax.fori_loop(0, OWN, turned, 0)
    pl.semaphore_wait(barrier, N_COLS - 1 + N_ROWS - 1)

    def remote(src, dst, send, recv, to):
        return pltpu.make_async_remote_copy(
            src_ref=src, dst_ref=dst, send_sem=send, recv_sem=recv, device_id=to, device_id_type=MESH)

    def step_of(s):
        return 1 if s == 0 else -1

    def half(h, s, f):
        return pl.ds(4 * h + 2 * (s if f == 0 else 1 - s), 2)

    def copy_a(j, h, s, f):
        cut = half(h, s, f)
        return remote(own.at[j, cut], gx.at[j, y, z, cut],
                      sa.at[j, h, s, f], ra.at[j, h, s, f], row_peer(1 - h, step_of(s)))

    def copy_b(j, h, s):
        yy, zz = yz(1 - h, -step_of(s))
        ref = gx.at[j, yy, zz, half(h, s, 0)]
        return remote(ref, ref, sb.at[j, h, s], rb.at[j, h, s], row_peer(1 - h, step_of(s)))

    def copy_c(j, h, s, f):
        cut = half(h, s, f)
        ref = gx.at[j, y, :, cut] if h == 0 else gx.at[j, :, z, cut]
        return remote(ref, ref, sc.at[j, h, s, f], rc.at[j, h, s, f], row_peer(h, step_of(s)))

    def copy_d(j, h, s):
        yy, zz = yz(h, -step_of(s))
        cut = half(h, s, 0)
        ref = gx.at[j, yy, :, cut] if h == 0 else gx.at[j, :, zz, cut]
        return remote(ref, ref, sd.at[j, h, s], rd.at[j, h, s], row_peer(h, step_of(s)))

    ways = [(h, s) for h in (0, 1) for s in (0, 1)]

    def do_a(j):
        for f in (0, 1):
            for h, s in ways:
                copy_a(j, h, s, f).start()

    def do_b(j):
        for h, s in ways:
            copy_a(j, h, s, 0).wait_recv()
            copy_b(j, h, s).start()

    def do_c(j):
        for h, s in ways:
            copy_a(j, h, s, 1).wait_recv()
        for h, s in ways:
            copy_b(j, h, s).wait_recv()
        for h, s in ways:
            copy_c(j, h, s, 0).start()

    def do_cc(j):
        for h, s in ways:
            copy_c(j, h, s, 1).start()

    def do_d(j):
        for h, s in ways:
            copy_c(j, h, s, 0).wait_recv()
            copy_d(j, h, s).start()

    def do_e(j):
        for h, s in ways:
            copy_c(j, h, s, 1).wait_recv()
            copy_d(j, h, s).wait_recv()

    def split(i, carry):
        slot = lax.rem(i, SLOTS)
        load(i, slot).wait()
        for k in range(STAGE):
            high, low = halves(jnp.transpose(stage[slot, k]))
            pairs[i * STAGE + k, 0:TILE] = high
            pairs[i * STAGE + k, TILE:2 * TILE] = low

        @pl.when(i + SLOTS < CAP // STAGE)
        def _():
            load(i + SLOTS, slot).start()

        return carry

    def spread(j):
        def one(g, carry):
            high, low = halves(gx[j, g // 32, lax.rem(g // 8, 4), lax.rem(g, 8)])
            xpair[g, 0:WIDTH, 0:TILE] = high
            xpair[g, 0:WIDTH, TILE:2 * TILE] = high
            xpair[g, WIDTH:2 * WIDTH, 0:TILE] = low
            xpair[g, WIDTH:2 * WIDTH, TILE:2 * TILE] = low
            return carry

        lax.fori_loop(0, N_ROWS * OWN, one, 0, unroll=8)

    def multiply(first, count, run):
        def group(g, run):
            for u in range(GROUP):
                t = first + g * GROUP + u
                both = jnp.dot(xpair[table[1, t]], pairs[table[0, t]], preferred_element_type=jnp.float32)
                run = run * table[2, t].astype(jnp.float32) + (both[:WIDTH] + both[WIDTH:])
                sums[t] = run
            return run

        return lax.fori_loop(0, count // GROUP, group, run)

    def collect(j):
        def one(i, carry):
            at = table[3, i]
            panel[j, i // 16, lax.rem(i // 8, 2), lax.rem(i, 8)] = jnp.where(
                at >= 0, sums[jnp.maximum(at, 0)], 0.0)
            return carry

        lax.fori_loop(0, PANEL, one, 0, unroll=8)

    def swap(j, off):
        at = turn(x, off)
        i = off % SIDE
        return remote(panel.at[j, at, 1 - q], near.at[j, at], se.at[j, i], re.at[j, i], partner)

    def copy_f(j, s):
        return remote(panel.at[j, turn(x, 2), q, pl.ds(4 * s, 4)], mid.at[j, s],
                      sf.at[j, s], rf.at[j, s], x_peer(step_of(s)))

    def copy_g(j, s, f):
        cut = pl.ds(4 * (1 - s if f == 0 else s), 4)
        return remote(panel.at[j, turn(x, step_of(s)), q, cut], far.at[j, s, cut],
                      sg.at[j, s, f], rg.at[j, s, f], x_peer(step_of(s)))

    offs = (2, 1, -1, 0)

    def do_p(j):
        collect(j)
        for off in offs:
            swap(j, off).start()

    def do_q(j):
        for off in offs:
            swap(j, off).wait_recv()
            at = turn(x, off)
            panel[j, at, q] = panel[j, at, q] + near[j, at]
            if off == 2:
                copy_f(j, 0).start()
                copy_f(j, 1).start()
            elif off != 0:
                copy_g(j, 0 if off == 1 else 1, 0).start()

    def do_r(j):
        for s in (0, 1):
            copy_f(j, s).wait_recv()
            at = turn(x, step_of(s))
            cut = pl.ds(4 * s, 4)
            panel[j, at, q, cut] = panel[j, at, q, cut] + mid[j, s]
            copy_g(j, s, 1).start()

    def do_s(j):
        for s in (0, 1):
            for f in (0, 1):
                copy_g(j, s, f).wait_recv()
        mats[1, :, j * WIDTH:(j + 1) * WIDTH, :] = panel[j, x, q] + (far[j, 0] + far[j, 1])

    def copy_h(p, d):
        to = lax.rem(c + d, N_COLS)
        return remote(share.at[p, to], got_cols.at[p, d], sh.at[p, d], rh.at[p, d], col_mate(d))

    def copy_i(p, d):
        return remote(slices.at[p], got_rows.at[p, r], si.at[p, d], ri.at[p, d], row_mate(d))

    def copy_j(p, d):
        return remote(grams.at[p, c], grams.at[p, c], sj.at[p, d], rj.at[p, d], col_mate(d))

    def sum_start(p, at):
        total = jnp.zeros((TILE, TILE), jnp.float32)
        for b in range(OWN):
            block = mats[at, b]
            total = total + exact(block, block, 1, 1)
        share[p] = total.reshape(N_COLS, SLICE, TILE)
        for d in range(1, N_COLS):
            copy_h(p, d).start()

    def sum_rows(p):
        for d in range(1, N_COLS):
            copy_h(p, d).wait_recv()
        part = share[p, c]
        for d in range(1, N_COLS):
            part = part + got_cols[p, d]
        slices[p] = part
        got_rows[p, r] = part
        for d in range(1, N_ROWS):
            copy_i(p, d).start()

    def sum_cols(p):
        for d in range(1, N_ROWS):
            copy_i(p, d).wait_recv()
        part = got_rows[p, 0]
        for d in range(1, N_ROWS):
            part = part + got_rows[p, d]
        grams[p, c] = part
        for d in range(1, N_COLS):
            copy_j(p, d).start()

    def sum_end(p):
        for d in range(1, N_COLS):
            copy_j(p, d).wait_recv()
        triangles(grams[p].reshape(TILE, TILE) / NODES, uppers.at[p], lowers.at[p], work)

    steps = CAP // STAGE

    def some(lo, hi):
        lax.fori_loop(lo, hi, split, 0)

    for j in range(PARTS):
        do_a(j)
    sum_start(0, 0)
    for copy in fetch[1:]:
        copy.wait()
    sort_slots(count[0, 0], rows_idx, cols_idx, plan)
    to_scalars = pltpu.make_async_copy(plan, table, table_sem)
    to_scalars.start()
    do_b(0)
    do_b(1)
    sum_rows(0)
    some(0, 4)
    do_b(2)
    do_b(3)
    do_c(0)
    do_cc(0)
    do_c(1)
    some(4, 16)
    sum_cols(0)
    some(16, 26)
    do_d(0)
    do_cc(1)
    do_c(2)
    some(26, steps)
    to_scalars.wait()
    sum_end(0)
    do_d(1)
    do_cc(2)
    do_c(3)
    do_e(0)

    zero = jnp.zeros((WIDTH, TILE), jnp.float32)
    cuts = (0, 80, 160, 240, 320)

    def part(j, between):
        spread(j)
        run = zero
        for k in range(4):
            run = multiply(cuts[k], cuts[k + 1] - cuts[k], run)
            for act, i in between[k]:
                act(i)

    part(0, [[], [], [], [(do_p, 0)]])
    do_d(2)
    do_cc(3)
    do_e(1)
    part(1, [[], [(do_q, 0)], [], [(do_p, 1)]])
    do_d(3)
    do_r(0)
    do_e(2)
    part(2, [[], [(do_q, 1)], [(do_s, 0)], [(do_p, 2)]])
    do_r(1)
    do_e(3)
    part(3, [[], [(do_q, 2)], [(do_s, 1)], [(do_r, 2), (do_p, 3)]])
    do_q(3)
    do_s(2)
    do_r(3)
    do_s(3)

    lower = lowers[0]
    for b in range(OWN):
        mats[2, b] = exact(lower, mats[1, b], 1, 0)
    store = [
        pltpu.make_async_copy(mats.at[1], plain, out_sem.at[0]),
        pltpu.make_async_copy(mats.at[2], scaled, out_sem.at[1]),
    ]
    for copy in store:
        copy.start()
    sum_start(1, 2)
    sum_rows(1)
    sum_cols(1)
    sum_end(1)
    upper[...] = uppers[...]
    inverse[...] = lowers[1]
    spread_of = jnp.sum(jnp.square(uppers[1]), keepdims=True) * jnp.sum(jnp.square(lowers[1]), keepdims=True)
    health[0, 0] = jnp.where(spread_of[0, 0] < SPREAD * TILE * TILE, 1, 0)
    for copy in store:
        copy.wait()

    for j in range(PARTS):
        for h, s in ways:
            for f in (0, 1):
                copy_a(j, h, s, f).wait_send()
                copy_c(j, h, s, f).wait_send()
            copy_b(j, h, s).wait_send()
            copy_d(j, h, s).wait_send()
        for off in offs:
            swap(j, off).wait_send()
        for s in (0, 1):
            copy_f(j, s).wait_send()
            copy_g(j, s, 0).wait_send()
            copy_g(j, s, 1).wait_send()
    for p in (0, 1):
        for d in range(1, N_COLS):
            copy_h(p, d).wait_send()
            copy_j(p, d).wait_send()
        for d in range(1, N_ROWS):
            copy_i(p, d).wait_send()


def finish_kernel(scaled, upper, inverse, basis, factor, first_factor):
    for b in range(OWN):
        basis[b] = jnp.transpose(exact(inverse[...], scaled[b], 1, 0))
    whole = exact(upper[1], upper[0], 1, 0)
    factor[...] = whole
    first_factor[...] = whole


def product(tiles, rows_idx, cols_idx, count, probes):
    scalar = pl.BlockSpec(memory_space=pltpu.SMEM)
    vector = pl.BlockSpec(memory_space=pltpu.VMEM)
    anywhere = pl.BlockSpec(memory_space=pl.ANY)
    f32, bf16 = jnp.float32, jnp.bfloat16
    piece = (OWN, WIDTH, TILE)
    square = (TILE, TILE)
    slab = (SLICE, TILE)
    return pl.pallas_call(
        product_kernel,
        out_shape=[
            jax.ShapeDtypeStruct((OWN,) + square, f32),
            jax.ShapeDtypeStruct((OWN,) + square, f32),
            jax.ShapeDtypeStruct((2,) + square, f32),
            jax.ShapeDtypeStruct(square, f32),
            jax.ShapeDtypeStruct((1, 1), jnp.int32),
        ],
        in_specs=[anywhere] * 5,
        out_specs=[anywhere] * 2 + [vector] * 2 + [scalar],
        scratch_shapes=[
            pltpu.SMEM((1, 1), jnp.int32),
            pltpu.VMEM((1, CAP), jnp.int32),
            pltpu.VMEM((1, CAP), jnp.int32),
            pltpu.VMEM((OWN,) + square, f32),
            pltpu.VMEM((PARTS,) + piece, f32),
            pltpu.VMEM((PARTS, SIDE, SIDE) + piece, f32),
            pltpu.VMEM((CAP, 2 * TILE, TILE), bf16),
            pltpu.VMEM((SLOTS, STAGE, TILE, TILE), f32),
            pltpu.VMEM((N_ROWS * OWN, 2 * WIDTH, 2 * TILE), bf16),
            pltpu.VMEM((CAP, WIDTH, TILE), f32),
            pltpu.VMEM((PARTS, SIDE, 2) + piece, f32),
            pltpu.VMEM((PARTS, SIDE) + piece, f32),
            pltpu.VMEM((PARTS, 2, OWN // 2, WIDTH, TILE), f32),
            pltpu.VMEM((PARTS, 2) + piece, f32),
            pltpu.VMEM((8, 3 * TILE), jnp.int32),
            pltpu.SMEM((8, 3 * TILE), jnp.int32),
            pltpu.VMEM((3, OWN) + square, f32),
            pltpu.VMEM((2, N_COLS) + slab, f32),
            pltpu.VMEM((2,) + slab, f32),
            pltpu.VMEM((2, N_COLS) + slab, f32),
            pltpu.VMEM((2, N_COLS) + slab, f32),
            pltpu.VMEM((2, N_ROWS) + slab, f32),
            pltpu.VMEM((TILE, 2 * TILE), f32),
            pltpu.VMEM((2,) + square, f32),
            pltpu.VMEM((2,) + square, f32),
            DMA((SLOTS,)),
        ]
        + [DMA((PARTS, 2, 2, 2))] * 2
        + [DMA((PARTS, 2, 2))] * 2
        + [DMA((PARTS, 2, 2, 2))] * 2
        + [DMA((PARTS, 2, 2))] * 2
        + [DMA((PARTS, SIDE))] * 2
        + [DMA((PARTS, 2))] * 2
        + [DMA((PARTS, 2, 2))] * 2
        + [DMA(()), DMA((4,)), DMA((2,))]
        + [DMA((2, N_COLS))] * 2
        + [DMA((2, N_ROWS))] * 2
        + [DMA((2, N_COLS))] * 2,
        compiler_params=pltpu.CompilerParams(
            collective_id=2, has_side_effects=True, vmem_limit_bytes=60 * 2**20),
        name="node_basis",
    )(count, rows_idx, cols_idx, tiles, probes.reshape((OWN,) + square))


def finish(scaled, upper, inverse):
    vector = pl.BlockSpec(memory_space=pltpu.VMEM)
    square = jax.ShapeDtypeStruct((TILE, TILE), jnp.float32)
    return pl.pallas_call(
        finish_kernel,
        out_shape=[jax.ShapeDtypeStruct(scaled.shape, jnp.float32), square, square],
        in_specs=[vector] * 3,
        out_specs=[vector] * 3,
        compiler_params=pltpu.CompilerParams(vmem_limit_bytes=16 * 2**20),
        name="finish",
    )(scaled, upper, inverse)


def signal_all(sem, r, c):
    def cols_peer(d, carry):
        pl.semaphore_signal(sem, inc=1, device_id=(r, lax.rem(c + d, N_COLS)), device_id_type=MESH)
        return carry

    def rows_peer(d, carry):
        pl.semaphore_signal(sem, inc=1, device_id=(lax.rem(r + d, N_ROWS), c), device_id_type=MESH)
        return carry

    lax.fori_loop(1, N_COLS, cols_peer, 0)
    lax.fori_loop(1, N_ROWS, rows_peer, 0)


def sum_kernel(g_ref, out_ref, part, got_a, got_b, send_a, recv_a, send_b, recv_b, send_c, recv_c):
    r, c = lax.axis_index("rows"), lax.axis_index("cols")
    barrier = pltpu.get_barrier_semaphore()
    signal_all(barrier, r, c)
    pl.semaphore_wait(barrier, N_COLS - 1 + N_ROWS - 1)

    def copy_a(d):
        to = lax.rem(c + d, N_COLS)
        return pltpu.make_async_remote_copy(
            src_ref=g_ref.at[to], dst_ref=got_a.at[d], send_sem=send_a.at[d], recv_sem=recv_a.at[d],
            device_id=(r, to), device_id_type=MESH)

    def copy_b(d):
        return pltpu.make_async_remote_copy(
            src_ref=part, dst_ref=got_b.at[r], send_sem=send_b.at[d], recv_sem=recv_b.at[d],
            device_id=(lax.rem(r + d, N_ROWS), c), device_id_type=MESH)

    def copy_c(d):
        return pltpu.make_async_remote_copy(
            src_ref=out_ref.at[c], dst_ref=out_ref.at[c], send_sem=send_c.at[d], recv_sem=recv_c.at[d],
            device_id=(r, lax.rem(c + d, N_COLS)), device_id_type=MESH)

    def each(copy, n, act):
        def step(d, carry):
            getattr(copy(d), act)()
            return carry

        lax.fori_loop(1, n, step, 0)

    each(copy_a, N_COLS, "start")
    each(copy_a, N_COLS, "wait_recv")
    total = g_ref[c]
    for d in range(1, N_COLS):
        total = total + got_a[d]
    part[...] = total
    got_b[r] = total
    each(copy_b, N_ROWS, "start")
    each(copy_a, N_COLS, "wait_send")
    each(copy_b, N_ROWS, "wait_recv")
    total = got_b[0]
    for d in range(1, N_ROWS):
        total = total + got_b[d]
    out_ref[c] = total
    each(copy_c, N_COLS, "start")
    each(copy_b, N_ROWS, "wait_send")
    each(copy_c, N_COLS, "wait")


def sum_everywhere(matrix, ident):
    size = matrix.shape[0]
    rows = size // N_COLS
    piece = (rows, size)
    out = pl.pallas_call(
        sum_kernel,
        out_shape=jax.ShapeDtypeStruct((N_COLS,) + piece, jnp.float32),
        in_specs=[pl.BlockSpec(memory_space=pltpu.VMEM)],
        out_specs=pl.BlockSpec(memory_space=pltpu.VMEM),
        scratch_shapes=[
            pltpu.VMEM(piece, jnp.float32),
            pltpu.VMEM((N_COLS,) + piece, jnp.float32),
            pltpu.VMEM((N_ROWS,) + piece, jnp.float32),
            DMA((N_COLS,)), DMA((N_COLS,)), DMA((N_ROWS,)), DMA((N_ROWS,)), DMA((N_COLS,)), DMA((N_COLS,)),
        ],
        compiler_params=pltpu.CompilerParams(collective_id=ident, has_side_effects=True),
        name="sum_everywhere",
    )(matrix.reshape((N_COLS,) + piece))
    return out.reshape(size, size)


def two_passes(matrix):
    def normal(value):
        gram = jnp.einsum("rk,rl->kl", value, value, precision=lax.Precision.HIGHEST)
        lower = jnp.linalg.cholesky(sum_everywhere(gram, 1) / NODES)
        inverse = jax.scipy.linalg.solve_triangular(
            lower, jnp.eye(TILE, dtype=jnp.float32), lower=True)
        return jnp.dot(value, inverse.T, precision=lax.Precision.HIGHEST), lower

    first, lower = normal(matrix)
    basis, lower_next = normal(first)
    return basis, jnp.dot(lower_next.T, lower.T, precision=lax.Precision.HIGHEST), lower.T


def shards(tile_values, tile_rows, tile_cols, tile_count, probes):
    plain, scaled, upper, inverse, health = product(
        tile_values[0, 0], tile_rows[0], tile_cols[0], tile_count, probes)

    def well():
        basis, factor, first_factor = finish(scaled, upper, inverse)
        return basis.reshape(probes.shape), factor, first_factor

    def ill():
        return two_passes(jnp.swapaxes(plain, 1, 2).reshape(probes.shape))

    return lax.cond(health[0, 0] != 0, well, ill)


def solution(mesh):
    placed = (
        P("rows", "cols", None, None, None),
        P("rows", "cols", None),
        P("rows", "cols", None),
        P("rows", "cols"),
        P(("rows", "cols"), None),
    )
    return jax.shard_map(
        shards,
        mesh=mesh,
        in_specs=placed,
        out_specs=(P(("rows", "cols"), None), P(), P()),
        check_vma=False,
    )
```

```python
import jax
import jax.numpy as jnp
from jax import lax
from jax.experimental import pallas as pl
from jax.experimental.pallas import tpu as pltpu
from jax.sharding import PartitionSpec as P

SIDE = 4
N_ROWS = SIDE * SIDE
N_COLS = 8
TILE = 128
CAP = 320
OWN = 8
PANEL = OWN * N_COLS
PARTS = 4
WIDTH = TILE // PARTS
GROUP = 40
STAGE = 8
STRIP = 16
HEAD = TILE - WIDTH
SLICE = TILE // N_COLS
SPREAD = 1.5
NODES = OWN * TILE * N_ROWS * N_COLS
SLOTS = 8
MESH = pl.DeviceIdType.MESH
DMA = pltpu.SemaphoreType.DMA


def halves(value):
    high = value.astype(jnp.bfloat16)
    low = (value - high.astype(jnp.float32)).astype(jnp.bfloat16)
    return high, low


def exact(left, right, at, to):
    return lax.dot_general(
        left, right, (((at,), (to,)), ((), ())), precision=lax.Precision.HIGHEST,
        preferred_element_type=jnp.float32)


def triangles(work, upper, inverse, first, end):
    rows = lax.broadcasted_iota(jnp.int32, (TILE, TILE), 0)
    cols = lax.broadcasted_iota(jnp.int32, (TILE, TILE), 1)
    shape = (STRIP, TILE)
    place = lax.broadcasted_iota(jnp.int32, shape, 0)
    for lo in range(first, end, STRIP):
        hi = lo + STRIP
        strip = work[lo:hi, 0:TILE]
        turned = work[lo:hi, TILE:2 * TILE]
        columns = [jnp.broadcast_to(strip[:, lo + j:lo + j + 1], shape) for j in range(STRIP)]
        for k in range(STRIP):
            scale = lax.rsqrt(jnp.broadcast_to(columns[k][k:k + 1], shape))
            weight = columns[k] * scale
            for j in range(k + 1, STRIP):
                columns[j] = columns[j] - weight * jnp.broadcast_to(weight[j:j + 1], shape)
            pivot = jnp.broadcast_to(strip[k:k + 1], shape) * scale
            other = jnp.broadcast_to(turned[k:k + 1], shape) * scale
            weight = jnp.where(place > k, weight, 0.0)
            strip = jnp.where(place == k, pivot, strip - weight * pivot)
            turned = jnp.where(place == k, other, turned - weight * other)
        strip = jnp.where(cols[lo:hi] >= rows[lo:hi], strip, 0.0)
        upper[lo:hi, :] = strip
        inverse[lo:hi, :] = turned
        if hi < TILE:
            change = exact(strip, jnp.concatenate([strip, turned], axis=1), 0, 0)
            work[hi:, :] = work[hi:, :] - change[hi:, :]


def with_identity(work, gram):
    rows = lax.broadcasted_iota(jnp.int32, (TILE, TILE), 0)
    cols = lax.broadcasted_iota(jnp.int32, (TILE, TILE), 1)
    work[:, 0:TILE] = gram
    work[:, TILE:2 * TILE] = jnp.where(rows == cols, 1.0, 0.0)


def last_columns(work, upper, inverse, gram):
    cols = lax.broadcasted_iota(jnp.int32, (HEAD, TILE), 1)
    turned = inverse[0:HEAD, :]
    side = jnp.where(cols >= HEAD, exact(turned, gram, 1, 0), 0.0)
    upper[0:HEAD, :] = upper[0:HEAD, :] + side
    change = exact(side, jnp.concatenate([side, turned], axis=1), 0, 0)
    rows = lax.broadcasted_iota(jnp.int32, (TILE - HEAD, TILE), 0) + HEAD
    below = lax.broadcasted_iota(jnp.int32, (TILE - HEAD, TILE), 1)
    work[HEAD:, 0:TILE] = gram[HEAD:, :] - change[HEAD:, 0:TILE]
    work[HEAD:, TILE:2 * TILE] = jnp.where(rows == below, 1.0, 0.0) - change[HEAD:, TILE:2 * TILE]


def sort_slots(count, rows_idx, cols_idx, plan):
    blocks = CAP // TILE + 1
    square = (TILE, TILE)
    lane = lax.broadcasted_iota(jnp.int32, (1, TILE), 1)
    high = lax.broadcasted_iota(jnp.int32, square, 0)
    wide = lax.broadcasted_iota(jnp.int32, square, 1)

    def block(ref, b):
        width = min(TILE, CAP - b * TILE)
        value = ref[:, b * TILE:b * TILE + width]
        if width < TILE:
            value = jnp.concatenate([value, jnp.zeros((1, TILE - width), jnp.int32)], axis=1)
        return value

    def down(value):
        return jnp.transpose(jnp.broadcast_to(value, square))

    def total(mask, value=1):
        return jnp.sum(jnp.where(mask, value, 0), axis=0, keepdims=True)

    slot = [lane + b * TILE for b in range(blocks)]
    row = [jnp.where(slot[b] < count, block(rows_idx, b), PANEL) for b in range(blocks)]
    row_down = [down(v) for v in row]
    place, packed = [], []
    for b in range(blocks):
        rank = jnp.zeros((1, TILE), jnp.int32)
        before = jnp.zeros((1, TILE), jnp.int32)
        for a in range(blocks):
            same = row_down[a] == row[b]
            if a == b:
                same = jnp.logical_and(same, high < wide)
            earlier = row_down[a] < row[b]
            if a <= b:
                earlier = jnp.logical_or(earlier, same)
                before = before + total(same)
            rank = rank + total(earlier)
        place.append(down(rank))
        goes_on = jnp.where(before > 0, 1, 0)
        packed.append(down((goes_on * blocks * TILE + slot[b]) * TILE + block(cols_idx, b)))
    for b in range(blocks):
        value = jnp.zeros((1, TILE), jnp.int32)
        for a in range(blocks):
            value = value + total(place[a] == wide + b * TILE, packed[a])
        rest = value // TILE
        cut = pl.ds(b * TILE, TILE)
        plan[0:1, cut] = rest % (blocks * TILE)
        plan[1:2, cut] = value % TILE
        plan[2:3, cut] = rest // (blocks * TILE)
        upto = jnp.zeros((1, TILE), jnp.int32)
        here = jnp.zeros((1, TILE), jnp.int32)
        for a in range(blocks):
            upto = upto + total(row_down[a] <= wide)
            here = here + total(row_down[a] == wide)
        plan[3:4, cut] = jnp.where(here > 0, upto - 1, -1)


def product_kernel(
    count_in, rows_in, cols_in, tiles, probes_in, plain, scaled, upper, inverse, health,
    count, rows_idx, cols_idx, probes, own, gx, pairs, stage, xpair, sums, panel, near, mid, far,
    plan, table, mats, share, slices, grams, got_cols, got_rows, work, uppers, lowers,
    stage_sem, sa, ra, sb, rb, sc, rc, sd, rd, se, re, sf, rf, sg, rg,
    table_sem, in_sem, out_sem, sh, rh, si, ri, sj, rj,
):
    r, c = lax.axis_index("rows"), lax.axis_index("cols")
    y, z = r // SIDE, lax.rem(r, SIDE)
    x, q = c // 2, lax.rem(c, 2)

    def turn(v, off):
        return lax.rem(v + off + SIDE, SIDE)

    def yz(dim, off):
        return (turn(y, off), z) if dim == 0 else (y, turn(z, off))

    def row_peer(dim, off):
        yy, zz = yz(dim, off)
        return (yy * SIDE + zz, c)

    def x_peer(off):
        return (r, turn(x, off) * 2 + q)

    partner = (r, x * 2 + 1 - q)

    def load(i, slot):
        return pltpu.make_async_copy(tiles.at[pl.ds(i * STAGE, STAGE)], stage.at[slot], stage_sem.at[slot])

    fetch = [
        pltpu.make_async_copy(src, dst, in_sem.at[i])
        for i, (src, dst) in enumerate(
            [(probes_in, probes), (rows_in, rows_idx), (cols_in, cols_idx), (count_in, count)])
    ]
    for copy in fetch:
        copy.start()

    barrier = pltpu.get_barrier_semaphore()

    def col_mate(d):
        return (r, lax.rem(c + d, N_COLS))

    def row_mate(d):
        return (lax.rem(r + d, N_ROWS), c)

    for d in range(1, N_COLS):
        pl.semaphore_signal(barrier, inc=1, device_id=col_mate(d), device_id_type=MESH)
    for d in range(1, N_ROWS):
        pl.semaphore_signal(barrier, inc=1, device_id=row_mate(d), device_id_type=MESH)

    for i in range(SLOTS):
        load(i, i).start()

    def turned(b, carry):
        block = jnp.transpose(probes[b])
        mats[0, b] = block
        for j in range(PARTS):
            own[j, b] = block[j * WIDTH:(j + 1) * WIDTH]
            gx[j, y, z, b] = block[j * WIDTH:(j + 1) * WIDTH]
        return carry

    fetch[0].wait()
    lax.fori_loop(0, OWN, turned, 0)
    pl.semaphore_wait(barrier, N_COLS - 1 + N_ROWS - 1)

    def remote(src, dst, send, recv, to):
        return pltpu.make_async_remote_copy(
            src_ref=src, dst_ref=dst, send_sem=send, recv_sem=recv, device_id=to, device_id_type=MESH)

    def step_of(s):
        return 1 if s == 0 else -1

    def half(h, s, f):
        return pl.ds(4 * h + 2 * (s if f == 0 else 1 - s), 2)

    def copy_a(j, h, s, f):
        cut = half(h, s, f)
        return remote(own.at[j, cut], gx.at[j, y, z, cut],
                      sa.at[j, h, s, f], ra.at[j, h, s, f], row_peer(1 - h, step_of(s)))

    def copy_b(j, h, s):
        yy, zz = yz(1 - h, -step_of(s))
        ref = gx.at[j, yy, zz, half(h, s, 0)]
        return remote(ref, ref, sb.at[j, h, s], rb.at[j, h, s], row_peer(1 - h, step_of(s)))

    def copy_c(j, h, s, f):
        cut = half(h, s, f)
        ref = gx.at[j, y, :, cut] if h == 0 else gx.at[j, :, z, cut]
        return remote(ref, ref, sc.at[j, h, s, f], rc.at[j, h, s, f], row_peer(h, step_of(s)))

    def copy_d(j, h, s):
        yy, zz = yz(h, -step_of(s))
        cut = half(h, s, 0)
        ref = gx.at[j, yy, :, cut] if h == 0 else gx.at[j, :, zz, cut]
        return remote(ref, ref, sd.at[j, h, s], rd.at[j, h, s], row_peer(h, step_of(s)))

    ways = [(h, s) for h in (0, 1) for s in (0, 1)]

    def do_a(j):
        for f in (0, 1):
            for h, s in ways:
                copy_a(j, h, s, f).start()

    def do_b(j):
        for h, s in ways:
            copy_a(j, h, s, 0).wait_recv()
            copy_b(j, h, s).start()

    def do_c(j):
        for h, s in ways:
            copy_a(j, h, s, 1).wait_recv()
        for h, s in ways:
            copy_b(j, h, s).wait_recv()
        for h, s in ways:
            copy_c(j, h, s, 0).start()

    def do_cc(j):
        for h, s in ways:
            copy_c(j, h, s, 1).start()

    def do_d(j):
        for h, s in ways:
            copy_c(j, h, s, 0).wait_recv()
            copy_d(j, h, s).start()

    def do_e(j):
        for h, s in ways:
            copy_c(j, h, s, 1).wait_recv()
            copy_d(j, h, s).wait_recv()

    def split(i, carry):
        slot = lax.rem(i, SLOTS)
        load(i, slot).wait()
        for k in range(STAGE):
            high, low = halves(jnp.transpose(stage[slot, k]))
            pairs[i * STAGE + k, 0:TILE] = high
            pairs[i * STAGE + k, TILE:2 * TILE] = low

        @pl.when(i + SLOTS < CAP // STAGE)
        def _():
            load(i + SLOTS, slot).start()

        return carry

    def spread(j):
        def one(g, carry):
            high, low = halves(gx[j, g // 32, lax.rem(g // 8, 4), lax.rem(g, 8)])
            xpair[g, 0:WIDTH, 0:TILE] = high
            xpair[g, 0:WIDTH, TILE:2 * TILE] = high
            xpair[g, WIDTH:2 * WIDTH, 0:TILE] = low
            xpair[g, WIDTH:2 * WIDTH, TILE:2 * TILE] = low
            return carry

        lax.fori_loop(0, N_ROWS * OWN, one, 0, unroll=8)

    def multiply(first, count, run):
        def group(g, run):
            for u in range(GROUP):
                t = first + g * GROUP + u
                both = jnp.dot(xpair[table[1, t]], pairs[table[0, t]], preferred_element_type=jnp.float32)
                run = run * table[2, t].astype(jnp.float32) + (both[:WIDTH] + both[WIDTH:])
                sums[t] = run
            return run

        return lax.fori_loop(0, count // GROUP, group, run)

    def collect(j):
        def one(i, carry):
            at = table[3, i]
            panel[j, i // 16, lax.rem(i // 8, 2), lax.rem(i, 8)] = jnp.where(
                at >= 0, sums[jnp.maximum(at, 0)], 0.0)
            return carry

        lax.fori_loop(0, PANEL, one, 0, unroll=8)

    def swap(j, off):
        at = turn(x, off)
        i = off % SIDE
        return remote(panel.at[j, at, 1 - q], near.at[j, at], se.at[j, i], re.at[j, i], partner)

    def copy_f(j, s):
        return remote(panel.at[j, turn(x, 2), q, pl.ds(4 * s, 4)], mid.at[j, s],
                      sf.at[j, s], rf.at[j, s], x_peer(step_of(s)))

    def copy_g(j, s, f):
        cut = pl.ds(4 * (1 - s if f == 0 else s), 4)
        return remote(panel.at[j, turn(x, step_of(s)), q, cut], far.at[j, s, cut],
                      sg.at[j, s, f], rg.at[j, s, f], x_peer(step_of(s)))

    offs = (2, 1, -1, 0)

    def do_p(j):
        collect(j)
        for off in offs:
            swap(j, off).start()

    def do_q(j):
        for off in offs:
            swap(j, off).wait_recv()
            at = turn(x, off)
            panel[j, at, q] = panel[j, at, q] + near[j, at]
            if off == 2:
                copy_f(j, 0).start()
                copy_f(j, 1).start()
            elif off != 0:
                copy_g(j, 0 if off == 1 else 1, 0).start()

    def do_r(j):
        for s in (0, 1):
            copy_f(j, s).wait_recv()
            at = turn(x, step_of(s))
            cut = pl.ds(4 * s, 4)
            panel[j, at, q, cut] = panel[j, at, q, cut] + mid[j, s]
            copy_g(j, s, 1).start()

    def do_s(j):
        for s in (0, 1):
            for f in (0, 1):
                copy_g(j, s, f).wait_recv()
        mats[1, :, j * WIDTH:(j + 1) * WIDTH, :] = panel[j, x, q] + (far[j, 0] + far[j, 1])

    def copy_h(p, d):
        to = lax.rem(c + d, N_COLS)
        return remote(share.at[p, to], got_cols.at[p, d], sh.at[p, d], rh.at[p, d], col_mate(d))

    def copy_i(p, d):
        return remote(slices.at[p], got_rows.at[p, r], si.at[p, d], ri.at[p, d], row_mate(d))

    def copy_j(p, d):
        return remote(grams.at[p, c], grams.at[p, c], sj.at[p, d], rj.at[p, d], col_mate(d))

    def sum_start(p, total):
        share[p] = total.reshape(N_COLS, SLICE, TILE)
        for d in range(1, N_COLS):
            copy_h(p, d).start()

    def own_gram(at, first, end):
        total = jnp.zeros((end - first, TILE), jnp.float32)
        for b in range(OWN):
            total = total + exact(mats[at, b, first:end, :], mats[at, b], 1, 1)
        return total

    def scale_rows(first, end):
        lower = lowers[0, first:end, :]
        for b in range(OWN):
            mats[2, b, first:end, :] = exact(lower, mats[1, b], 1, 0)

    def sum_rows(p):
        for d in range(1, N_COLS):
            copy_h(p, d).wait_recv()
        part = share[p, c]
        for d in range(1, N_COLS):
            part = part + got_cols[p, d]
        slices[p] = part
        got_rows[p, r] = part
        for d in range(1, N_ROWS):
            copy_i(p, d).start()

    def sum_cols(p):
        for d in range(1, N_ROWS):
            copy_i(p, d).wait_recv()
        part = got_rows[p, 0]
        for d in range(1, N_ROWS):
            part = part + got_rows[p, d]
        grams[p, c] = part
        for d in range(1, N_COLS):
            copy_j(p, d).start()

    def sum_end(p):
        for d in range(1, N_COLS):
            copy_j(p, d).wait_recv()
        return grams[p].reshape(TILE, TILE) / NODES

    steps = CAP // STAGE

    def some(lo, hi):
        lax.fori_loop(lo, hi, split, 0)

    for j in range(PARTS):
        do_a(j)
    sum_start(0, own_gram(0, 0, TILE))
    mats[1, :, HEAD:, :] = jnp.zeros((OWN, WIDTH, TILE), jnp.float32)
    mats[2, :, HEAD:, :] = jnp.zeros((OWN, WIDTH, TILE), jnp.float32)
    for copy in fetch[1:]:
        copy.wait()
    sort_slots(count[0, 0], rows_idx, cols_idx, plan)
    to_scalars = pltpu.make_async_copy(plan, table, table_sem)
    to_scalars.start()
    do_b(0)
    do_b(1)
    sum_rows(0)
    some(0, 4)
    do_b(2)
    do_b(3)
    do_c(0)
    do_cc(0)
    do_c(1)
    some(4, 16)
    sum_cols(0)
    some(16, 26)
    do_d(0)
    do_cc(1)
    do_c(2)
    some(26, steps)
    to_scalars.wait()
    with_identity(work, sum_end(0))
    triangles(work, uppers.at[0], lowers.at[0], 0, TILE)
    do_d(1)
    do_cc(2)
    do_c(3)
    do_e(0)

    zero = jnp.zeros((WIDTH, TILE), jnp.float32)
    cuts = (0, 80, 160, 240, 320)

    def part(j, between):
        spread(j)
        run = zero
        for k in range(4):
            run = multiply(cuts[k], cuts[k + 1] - cuts[k], run)
            for act, i in between[k]:
                act(i)

    part(0, [[], [], [], [(do_p, 0)]])
    do_d(2)
    do_cc(3)
    do_e(1)
    part(1, [[], [(do_q, 0)], [], [(do_p, 1)]])
    do_d(3)
    do_r(0)
    do_e(2)
    part(2, [[], [(do_q, 1)], [(do_s, 0)], [(do_p, 2)]])
    do_r(1)
    do_e(3)
    part(3, [[], [(do_q, 2)], [(do_s, 1)], [(do_r, 2), (do_p, 3)]])
    do_q(3)
    do_s(2)
    scale_rows(0, HEAD)
    blank = jnp.zeros((WIDTH, TILE), jnp.float32)
    sum_start(1, jnp.concatenate([own_gram(2, 0, HEAD), blank], axis=0))
    do_r(3)
    sum_rows(1)
    do_s(3)
    scale_rows(HEAD, TILE)
    low = own_gram(2, HEAD, TILE)
    head = jnp.zeros((HEAD, TILE), jnp.float32)
    low = jnp.concatenate([head, low], axis=0)
    rows = lax.broadcasted_iota(jnp.int32, (TILE, TILE), 0)
    sum_start(2, jnp.where(rows < HEAD, jnp.transpose(low), low))
    store = [
        pltpu.make_async_copy(mats.at[1], plain, out_sem.at[0]),
        pltpu.make_async_copy(mats.at[2], scaled, out_sem.at[1]),
    ]
    for copy in store:
        copy.start()
    sum_cols(1)
    sum_rows(2)
    with_identity(work, sum_end(1))
    triangles(work, uppers.at[1], lowers.at[1], 0, HEAD // 2)
    sum_cols(2)
    triangles(work, uppers.at[1], lowers.at[1], HEAD // 2, HEAD)
    last_columns(work, uppers.at[1], lowers.at[1], sum_end(2))
    triangles(work, uppers.at[1], lowers.at[1], HEAD, TILE)
    upper[...] = uppers[...]
    inverse[...] = lowers[1]
    spread_of = jnp.sum(jnp.square(uppers[1]), keepdims=True) * jnp.sum(jnp.square(lowers[1]), keepdims=True)
    health[0, 0] = jnp.where(spread_of[0, 0] < SPREAD * TILE * TILE, 1, 0)
    for copy in store:
        copy.wait()

    for j in range(PARTS):
        for h, s in ways:
            for f in (0, 1):
                copy_a(j, h, s, f).wait_send()
                copy_c(j, h, s, f).wait_send()
            copy_b(j, h, s).wait_send()
            copy_d(j, h, s).wait_send()
        for off in offs:
            swap(j, off).wait_send()
        for s in (0, 1):
            copy_f(j, s).wait_send()
            copy_g(j, s, 0).wait_send()
            copy_g(j, s, 1).wait_send()
    for p in (0, 1, 2):
        for d in range(1, N_COLS):
            copy_h(p, d).wait_send()
            copy_j(p, d).wait_send()
        for d in range(1, N_ROWS):
            copy_i(p, d).wait_send()


def finish_kernel(scaled, upper, inverse, basis, factor, first_factor):
    for b in range(OWN):
        basis[b] = jnp.transpose(exact(inverse[...], scaled[b], 1, 0))
    whole = exact(upper[1], upper[0], 1, 0)
    factor[...] = whole
    first_factor[...] = whole


def product(tiles, rows_idx, cols_idx, count, probes):
    scalar = pl.BlockSpec(memory_space=pltpu.SMEM)
    vector = pl.BlockSpec(memory_space=pltpu.VMEM)
    anywhere = pl.BlockSpec(memory_space=pl.ANY)
    f32, bf16 = jnp.float32, jnp.bfloat16
    piece = (OWN, WIDTH, TILE)
    square = (TILE, TILE)
    slab = (SLICE, TILE)
    return pl.pallas_call(
        product_kernel,
        out_shape=[
            jax.ShapeDtypeStruct((OWN,) + square, f32),
            jax.ShapeDtypeStruct((OWN,) + square, f32),
            jax.ShapeDtypeStruct((2,) + square, f32),
            jax.ShapeDtypeStruct(square, f32),
            jax.ShapeDtypeStruct((1, 1), jnp.int32),
        ],
        in_specs=[anywhere] * 5,
        out_specs=[anywhere] * 2 + [vector] * 2 + [scalar],
        scratch_shapes=[
            pltpu.SMEM((1, 1), jnp.int32),
            pltpu.VMEM((1, CAP), jnp.int32),
            pltpu.VMEM((1, CAP), jnp.int32),
            pltpu.VMEM((OWN,) + square, f32),
            pltpu.VMEM((PARTS,) + piece, f32),
            pltpu.VMEM((PARTS, SIDE, SIDE) + piece, f32),
            pltpu.VMEM((CAP, 2 * TILE, TILE), bf16),
            pltpu.VMEM((SLOTS, STAGE, TILE, TILE), f32),
            pltpu.VMEM((N_ROWS * OWN, 2 * WIDTH, 2 * TILE), bf16),
            pltpu.VMEM((CAP, WIDTH, TILE), f32),
            pltpu.VMEM((PARTS, SIDE, 2) + piece, f32),
            pltpu.VMEM((PARTS, SIDE) + piece, f32),
            pltpu.VMEM((PARTS, 2, OWN // 2, WIDTH, TILE), f32),
            pltpu.VMEM((PARTS, 2) + piece, f32),
            pltpu.VMEM((8, 3 * TILE), jnp.int32),
            pltpu.SMEM((8, 3 * TILE), jnp.int32),
            pltpu.VMEM((3, OWN) + square, f32),
            pltpu.VMEM((3, N_COLS) + slab, f32),
            pltpu.VMEM((3,) + slab, f32),
            pltpu.VMEM((3, N_COLS) + slab, f32),
            pltpu.VMEM((3, N_COLS) + slab, f32),
            pltpu.VMEM((3, N_ROWS) + slab, f32),
            pltpu.VMEM((TILE, 2 * TILE), f32),
            pltpu.VMEM((2,) + square, f32),
            pltpu.VMEM((2,) + square, f32),
            DMA((SLOTS,)),
        ]
        + [DMA((PARTS, 2, 2, 2))] * 2
        + [DMA((PARTS, 2, 2))] * 2
        + [DMA((PARTS, 2, 2, 2))] * 2
        + [DMA((PARTS, 2, 2))] * 2
        + [DMA((PARTS, SIDE))] * 2
        + [DMA((PARTS, 2))] * 2
        + [DMA((PARTS, 2, 2))] * 2
        + [DMA(()), DMA((4,)), DMA((2,))]
        + [DMA((3, N_COLS))] * 2
        + [DMA((3, N_ROWS))] * 2
        + [DMA((3, N_COLS))] * 2,
        compiler_params=pltpu.CompilerParams(
            collective_id=2, has_side_effects=True, vmem_limit_bytes=60 * 2**20),
        name="node_basis",
    )(count, rows_idx, cols_idx, tiles, probes.reshape((OWN,) + square))


def finish(scaled, upper, inverse):
    vector = pl.BlockSpec(memory_space=pltpu.VMEM)
    square = jax.ShapeDtypeStruct((TILE, TILE), jnp.float32)
    return pl.pallas_call(
        finish_kernel,
        out_shape=[jax.ShapeDtypeStruct(scaled.shape, jnp.float32), square, square],
        in_specs=[vector] * 3,
        out_specs=[vector] * 3,
        compiler_params=pltpu.CompilerParams(vmem_limit_bytes=16 * 2**20),
        name="finish",
    )(scaled, upper, inverse)


def signal_all(sem, r, c):
    def cols_peer(d, carry):
        pl.semaphore_signal(sem, inc=1, device_id=(r, lax.rem(c + d, N_COLS)), device_id_type=MESH)
        return carry

    def rows_peer(d, carry):
        pl.semaphore_signal(sem, inc=1, device_id=(lax.rem(r + d, N_ROWS), c), device_id_type=MESH)
        return carry

    lax.fori_loop(1, N_COLS, cols_peer, 0)
    lax.fori_loop(1, N_ROWS, rows_peer, 0)


def sum_kernel(g_ref, out_ref, part, got_a, got_b, send_a, recv_a, send_b, recv_b, send_c, recv_c):
    r, c = lax.axis_index("rows"), lax.axis_index("cols")
    barrier = pltpu.get_barrier_semaphore()
    signal_all(barrier, r, c)
    pl.semaphore_wait(barrier, N_COLS - 1 + N_ROWS - 1)

    def copy_a(d):
        to = lax.rem(c + d, N_COLS)
        return pltpu.make_async_remote_copy(
            src_ref=g_ref.at[to], dst_ref=got_a.at[d], send_sem=send_a.at[d], recv_sem=recv_a.at[d],
            device_id=(r, to), device_id_type=MESH)

    def copy_b(d):
        return pltpu.make_async_remote_copy(
            src_ref=part, dst_ref=got_b.at[r], send_sem=send_b.at[d], recv_sem=recv_b.at[d],
            device_id=(lax.rem(r + d, N_ROWS), c), device_id_type=MESH)

    def copy_c(d):
        return pltpu.make_async_remote_copy(
            src_ref=out_ref.at[c], dst_ref=out_ref.at[c], send_sem=send_c.at[d], recv_sem=recv_c.at[d],
            device_id=(r, lax.rem(c + d, N_COLS)), device_id_type=MESH)

    def each(copy, n, act):
        def step(d, carry):
            getattr(copy(d), act)()
            return carry

        lax.fori_loop(1, n, step, 0)

    each(copy_a, N_COLS, "start")
    each(copy_a, N_COLS, "wait_recv")
    total = g_ref[c]
    for d in range(1, N_COLS):
        total = total + got_a[d]
    part[...] = total
    got_b[r] = total
    each(copy_b, N_ROWS, "start")
    each(copy_a, N_COLS, "wait_send")
    each(copy_b, N_ROWS, "wait_recv")
    total = got_b[0]
    for d in range(1, N_ROWS):
        total = total + got_b[d]
    out_ref[c] = total
    each(copy_c, N_COLS, "start")
    each(copy_b, N_ROWS, "wait_send")
    each(copy_c, N_COLS, "wait")


def sum_everywhere(matrix, ident):
    size = matrix.shape[0]
    rows = size // N_COLS
    piece = (rows, size)
    out = pl.pallas_call(
        sum_kernel,
        out_shape=jax.ShapeDtypeStruct((N_COLS,) + piece, jnp.float32),
        in_specs=[pl.BlockSpec(memory_space=pltpu.VMEM)],
        out_specs=pl.BlockSpec(memory_space=pltpu.VMEM),
        scratch_shapes=[
            pltpu.VMEM(piece, jnp.float32),
            pltpu.VMEM((N_COLS,) + piece, jnp.float32),
            pltpu.VMEM((N_ROWS,) + piece, jnp.float32),
            DMA((N_COLS,)), DMA((N_COLS,)), DMA((N_ROWS,)), DMA((N_ROWS,)), DMA((N_COLS,)), DMA((N_COLS,)),
        ],
        compiler_params=pltpu.CompilerParams(collective_id=ident, has_side_effects=True),
        name="sum_everywhere",
    )(matrix.reshape((N_COLS,) + piece))
    return out.reshape(size, size)


def two_passes(matrix):
    def normal(value):
        gram = jnp.einsum("rk,rl->kl", value, value, precision=lax.Precision.HIGHEST)
        lower = jnp.linalg.cholesky(sum_everywhere(gram, 1) / NODES)
        inverse = jax.scipy.linalg.solve_triangular(
            lower, jnp.eye(TILE, dtype=jnp.float32), lower=True)
        return jnp.dot(value, inverse.T, precision=lax.Precision.HIGHEST), lower

    first, lower = normal(matrix)
    basis, lower_next = normal(first)
    return basis, jnp.dot(lower_next.T, lower.T, precision=lax.Precision.HIGHEST), lower.T


def shards(tile_values, tile_rows, tile_cols, tile_count, probes):
    plain, scaled, upper, inverse, health = product(
        tile_values[0, 0], tile_rows[0], tile_cols[0], tile_count, probes)

    def well():
        basis, factor, first_factor = finish(scaled, upper, inverse)
        return basis.reshape(probes.shape), factor, first_factor

    def ill():
        return two_passes(jnp.swapaxes(plain, 1, 2).reshape(probes.shape))

    return lax.cond(health[0, 0] != 0, well, ill)


def solution(mesh):
    placed = (
        P("rows", "cols", None, None, None),
        P("rows", "cols", None),
        P("rows", "cols", None),
        P("rows", "cols"),
        P(("rows", "cols"), None),
    )
    return jax.shard_map(
        shards,
        mesh=mesh,
        in_specs=placed,
        out_specs=(P(("rows", "cols"), None), P(), P()),
        check_vma=False,
    )
```
